512 devices in a mesh: dp: 128 (over z, y, core), grp: 4 (over x).
Axes of the slice: x: 4, y: 8, z: 8, core: 2. Of those that a mesh axis runs over, the one named last changes fastest.
Arguments:
- embeddings: bfloat16 [65536, 768], P(('dp', 'grp')), may hold values from -6 to 6
- inv_temp: bfloat16 [65536], P(('dp', 'grp')), may hold values from 4 to 16
- cluster: int32 [65536, 1], P(('dp', 'grp')), may hold values from 0 to 127; in each aligned block of 128 rows (0 to 127, 128 to 255, ...) at most 2 rows name the same one
Outputs:
- neighbour: bfloat16 [65536, 768], P(('dp', 'grp'))
- duplicate_mass: bfloat16 [65536], P(('dp', 'grp'))
The draws below stay inside these ranges and needn't reach their ends.
Inputs may be any that keep to these rules, and one draw needn't show every extreme that they name: Among the 128 rows of one device no cluster is named more than 2 times, a bound that some block reaches.
All inputs are finite; a program needn't handle non-finite values.
Results may differ from the reference program's by a relative error of at most 0.011.
Values may be sent and summed in bfloat16 or wider, within the bound.
No kernel may reach another device: no remote copies, remote signals or barrier semaphores. Data moves between devices by JAX's collectives and lax.ppermute only.
A program may use at most 64 MiB of HBM per device.

```python
import math
import jax
import jax.numpy as jnp
import numpy as np
from jax import lax

D = 768
ROWS_DEV = 128
ROWS = 65536
CAP = 2
N_DP = 128
N_GRP = 4


def level_of(stream_key, dims, pieces, least, top_value):
    level, own = 1.0, jax.random.fold_in(stream_key, 6)
    for position, blocks in pieces:
        steps = jnp.exp(jax.random.uniform(jax.random.fold_in(own, position), (blocks,), jnp.float32, least / len(pieces), top_value / len(pieces)))
        level = level * jnp.repeat(steps, dims[position] // blocks).reshape([-1 if axis == position else 1 for axis in range(len(dims))])
    return level


def deal_out(own_key, own, number, rows, number_of, top, reach, skew):
    ranking = jax.random.permutation(own_key, number_of)
    heavy_load, ordinary = load_shares(number_of, rows * top, reach, skew, True), load_shares(number_of, rows * top, reach, skew, False)
    places = jnp.arange(number_of)

    def named(lengths, offset_by):
        used = int((lengths > 0).sum())
        fixed = max(1, used // 4)
        passed = fixed + (places - fixed + offset_by * (used - fixed)) % max(1, number_of - fixed)
        return jnp.zeros((number_of,), jnp.int32).at[ranking[jnp.where(places < fixed, places, passed)]].set(jnp.asarray(lengths, jnp.int32))

    lengths = jnp.where(number % 4 == 0, named(heavy_load, number // 4), named(ordinary, number - number // 4 - 1))
    mixed = jax.random.permutation(jax.random.fold_in(own, 3), number_of)
    source_of, receiver = mixed[0:number_of // 2 * 2:2], mixed[1:number_of // 2 * 2:2]
    slack = jnp.minimum(lengths[source_of] - 1, reach - lengths[receiver]) // 2
    slack = jnp.where((source_of == ranking[0]) | (receiver == ranking[0]) | (lengths[receiver] == 0), 0, jnp.maximum(slack, 0))
    passed = jax.random.randint(jax.random.fold_in(own, 4), (number_of // 2,), 0, 1 << 20) % (slack + 1)
    lengths = lengths.at[source_of].add(-passed).at[receiver].add(passed)
    items = jnp.searchsorted(jnp.cumsum(lengths), jnp.arange(rows * top), side="right").astype(jnp.int32)
    listing = items.reshape(top, rows).T
    listing = listing[jax.random.permutation(jax.random.fold_in(own, 1), rows)]
    offset_by = jax.random.randint(jax.random.fold_in(own, 2), (rows, 1), 0, top)
    return jnp.take_along_axis(listing, (jnp.arange(top)[None, :] + offset_by) % top, axis=1)


def load_shares(amount, total, bound, skew, full):
    loads = [(1 << 20) // math.isqrt(grade ** skew) + 1 for grade in range(1, amount + 1)]
    largest = bound if full else min(bound, max(-(-total // amount), total * loads[0] // sum(loads)))
    least = 1 if total - largest >= amount - 1 else 0
    given, rest = [largest] + [least] * (amount - 1), total - largest - least * (amount - 1)
    while rest > 0:
        movable = [i for i in range(1, amount) if given[i] < largest] or [i for i in range(1, amount) if given[i] < bound]
        whole, budget = sum([loads[i] for i in movable]), rest
        for i in movable:
            addition = min(bound - given[i], max(1, budget * loads[i] // whole), rest)
            given[i] = given[i] + addition
            rest = rest - addition
    return np.array(given)


def gaussian(rng, shape, scale, reach, split=(), held_as=jnp.bfloat16):
    factor_of = level_of(rng, shape, split, -0.22, 0.18) if split else 1.0
    array = jax.random.normal(rng, shape, jnp.float32) * scale * factor_of
    return jnp.minimum(jnp.maximum(array, -reach), reach).astype(held_as)


def setup_inputs(seed: int = 0) -> dict:
    streams_of = jax.random.split(jax.random.key(seed), 4)
    embeddings = gaussian(streams_of[0], (ROWS, D), 1.0, 6.0, ((0, 512),))
    inv_temp = jnp.clip(jnp.exp(math.log(16.0) - 1.3862944 * jax.random.uniform(streams_of[1], (ROWS,), jnp.float32) ** level_of(streams_of[1], (ROWS,), ((0, 512),), -0.2, 0.2)), 4.0, 16.0).astype(jnp.bfloat16)
    cluster_keys = jax.random.split(jax.random.fold_in(streams_of[2], 1), ROWS // ROWS_DEV)
    cluster_turns = jax.random.permutation(jax.random.fold_in(streams_of[2], 3), ROWS // ROWS_DEV)
    cluster = jax.vmap(lambda own, number: deal_out(jax.random.fold_in(streams_of[2], 2), own, number, ROWS_DEV, N_DP, 1, CAP, 2))(cluster_keys, cluster_turns).reshape((ROWS, 1))
    return {"embeddings": embeddings, "inv_temp": inv_temp, "cluster": cluster}


NEIGH_SCALE = 8.0

def normalize(embeddings):
    values = embeddings.astype(jnp.float32)
    square_mean = lax.optimization_barrier(jnp.mean(values * values, axis=1, keepdims=True))
    return (values * lax.rsqrt(square_mean + 1e-06) * (1.0 / math.sqrt(embeddings.shape[1]))).astype(jnp.bfloat16)

def reference(embeddings, inv_temp, cluster):
    unit_rows = normalize(embeddings)
    clusters = cluster[:, 0].astype(jnp.int32)
    sorted_index = jnp.argsort(clusters, stable=True).astype(jnp.int32)
    sorted_unit = unit_rows[sorted_index]
    sorted_temp = inv_temp.astype(jnp.float32)[sorted_index]
    sorted_cluster = clusters[sorted_index]
    counts = jnp.bincount(clusters, length=N_DP).astype(jnp.int32)
    starts = (jnp.cumsum(counts) - counts).astype(jnp.int32)
    widest = N_GRP * N_DP * CAP
    padded_unit = jnp.concatenate([sorted_unit, jnp.zeros((widest, D), jnp.bfloat16)], axis=0)
    padded_temp = jnp.concatenate([sorted_temp, jnp.zeros((widest,), jnp.float32)], axis=0)

    def cluster_tile(which):
        first = starts[which]
        members = counts[which]
        block_unit = lax.dynamic_slice_in_dim(padded_unit, first, widest, 0)
        block_temp = lax.dynamic_slice_in_dim(padded_temp, first, widest, 0)
        member_index = jnp.arange(widest, dtype=jnp.int32)
        present = member_index < members
        cosine = lax.dot_general(block_unit, block_unit, (((1,), (1,)), ((), ())), preferred_element_type=jnp.float32)
        temper = (block_temp[:, None] + block_temp[None, :]) * 0.5
        allowed = present[None, :] & (member_index[:, None] != member_index[None, :])
        tile_weight = jnp.where(allowed, jnp.exp((cosine - 1.0) * temper), 0.0)
        mass = lax.optimization_barrier(jnp.sum(tile_weight, axis=1))
        near_sum = jnp.dot(tile_weight.astype(jnp.bfloat16), block_unit, preferred_element_type=jnp.float32)
        neigh = (NEIGH_SCALE * math.sqrt(D) * near_sum / (1.0 + mass)[:, None]).astype(jnp.bfloat16)
        return (neigh, mass.astype(jnp.bfloat16))
    neighs, masses = lax.map(cluster_tile, jnp.arange(N_DP, dtype=jnp.int32))
    positions = jnp.arange(ROWS, dtype=jnp.int32)
    offset_in = positions - starts[sorted_cluster]
    sorted_neigh = neighs[sorted_cluster, offset_in]
    sorted_mass = masses[sorted_cluster, offset_in]
    neighbour = jnp.zeros((ROWS, D), jnp.bfloat16).at[sorted_index].set(sorted_neigh)
    duplicate_mass = jnp.zeros((ROWS,), jnp.bfloat16).at[sorted_index].set(sorted_mass)
    return (neighbour, duplicate_mass)
```

```python
import functools
import math

import jax
import jax.numpy as jnp
from jax import lax
from jax.experimental import pallas as pl
from jax.experimental.pallas import tpu as pltpu
from jax.sharding import Mesh
from jax.sharding import PartitionSpec as P

NEIGH_SCALE = 8.0
EXT = 128
NT = (((1,), (1,)), ((), ()))

AXES = ("z", "y", "core", "xhi", "xlo")
SPREAD = ("z", "y", "xhi")


def params():
    return pltpu.CompilerParams(vmem_limit_bytes=32 * 1024 * 1024)


def lane_to_row(ext):
    first = (lax.broadcasted_iota(jnp.int32, (16, EXT), 1) == 0).astype(jnp.bfloat16)
    return lax.dot_general(first, ext, NT, preferred_element_type=jnp.float32)[:1]


def pack_kernel(emb_ref, temp_ref, cluster_ref, send_ref, pick_ref):
    rows, width = emb_ref.shape
    slots = send_ref.shape[0]
    values = emb_ref[...].astype(jnp.float32)
    square_mean = jnp.mean(values * values, axis=1, keepdims=True)
    unit = (values * lax.rsqrt(square_mean + 1e-06) * (1.0 / math.sqrt(width))).astype(jnp.bfloat16)

    cluster_row = cluster_ref[...].astype(jnp.float32)
    row = lax.broadcasted_iota(jnp.int32, (rows, rows), 0)
    col = lax.broadcasted_iota(jnp.int32, (rows, rows), 1)
    cluster_col = jnp.sum(jnp.where(row == col, cluster_row, 0.0), axis=1, keepdims=True)
    same = cluster_row == cluster_col
    rank_row = jnp.sum(jnp.where(same & (row < col), 1.0, 0.0), axis=0, keepdims=True)
    rank_col = jnp.sum(jnp.where(same & (col < row), 1.0, 0.0), axis=1, keepdims=True)
    slot_row = (2.0 * cluster_row + rank_row).astype(jnp.int32)
    slot_col = (2.0 * cluster_col + rank_col).astype(jnp.int32)

    put = lax.broadcasted_iota(jnp.int32, (slots, rows), 0) == slot_row
    placed = jnp.dot(
        jnp.where(put, 1.0, 0.0).astype(jnp.bfloat16), unit, preferred_element_type=jnp.float32
    )
    temp = jnp.sum(jnp.where(put, temp_ref[...].astype(jnp.float32), 0.0), axis=1, keepdims=True)
    send_ref[:, :width] = placed.astype(jnp.bfloat16)
    send_ref[:, width:] = jnp.broadcast_to(temp, (slots, EXT)).astype(jnp.bfloat16)
    pick = lax.broadcasted_iota(jnp.int32, (rows, slots), 1) == slot_col
    pick_ref[...] = jnp.where(pick, 1.0, 0.0).astype(jnp.bfloat16)


def weigh(query_ref, key_ref, own_start):
    width = query_ref.shape[1] - EXT
    unit = key_ref[:, :width]
    cosine = lax.dot_general(
        query_ref[:, :width], unit, NT, preferred_element_type=jnp.float32
    )
    key_temp = lane_to_row(key_ref[:, width:])
    query_temp = query_ref[:, width : width + 1].astype(jnp.float32)
    weight = jnp.exp((cosine - 1.0) * ((query_temp + key_temp) * 0.5))
    allowed = key_temp > 0.0
    if own_start is not None:
        query_index = lax.broadcasted_iota(jnp.int32, cosine.shape, 0) + own_start
        allowed = allowed & (query_index != lax.broadcasted_iota(jnp.int32, cosine.shape, 1))
    weight = jnp.where(allowed, weight, 0.0)
    near = jnp.dot(weight.astype(jnp.bfloat16), unit, preferred_element_type=jnp.float32)
    return jnp.sum(weight, axis=1, keepdims=True), near


def first_kernel(core_ref, query_ref, key_ref, mass_ref, near_ref):
    mass, near = weigh(query_ref, key_ref, core_ref[0] * query_ref.shape[0])
    mass_ref[...] = jnp.broadcast_to(mass, mass_ref.shape)
    near_ref[...] = near


def second_kernel(query_ref, key_ref, mass_ref, near_ref, out_ref):
    width = near_ref.shape[1]
    mass, near = weigh(query_ref, key_ref, None)
    mass = mass + mass_ref[:, :1]
    near = near + near_ref[...]
    neigh = NEIGH_SCALE * math.sqrt(width) * near / (1.0 + mass)
    out_ref[:, :width] = neigh.astype(jnp.bfloat16)
    out_ref[:, width:] = jnp.broadcast_to(mass, (mass.shape[0], EXT)).astype(jnp.bfloat16)


def unpack_kernel(pick_ref, back_ref, neigh_ref, mass_ref):
    width = neigh_ref.shape[1]
    rows = jnp.dot(pick_ref[...], back_ref[...], preferred_element_type=jnp.float32)
    rows = rows.astype(jnp.bfloat16)
    neigh_ref[...] = rows[:, :width]
    mass_ref[...] = lane_to_row(rows[:, width:]).astype(jnp.bfloat16)


def call(kernel, outs, flops, *args, scalars=0):
    shapes = [jax.ShapeDtypeStruct(shape, dtype) for shape, dtype in outs]
    specs = [pl.BlockSpec(memory_space=pltpu.SMEM)] * scalars
    specs += [pl.BlockSpec(memory_space=pltpu.VMEM)] * (len(args) - scalars)
    moved = sum(a.size * a.dtype.itemsize for a in args)
    moved += sum(math.prod(s.shape) * s.dtype.itemsize for s in shapes)
    return pl.pallas_call(
        kernel,
        out_shape=shapes,
        in_specs=specs,
        out_specs=[pl.BlockSpec(memory_space=pltpu.VMEM)] * len(shapes),
        compiler_params=params(),
        cost_estimate=pl.CostEstimate(flops=flops, bytes_accessed=moved, transcendentals=0),
    )(*args)


def spread(slots, parts):
    count, wide = slots.shape
    moved = lax.all_to_all(
        slots.reshape(parts, count // parts, wide), SPREAD, split_axis=0, concat_axis=0, tiled=True
    )
    return moved.reshape(count, wide)


def shards(embeddings, inv_temp, cluster):
    rows, width = embeddings.shape
    parts = lax.axis_size("z") * lax.axis_size("y") * lax.axis_size("xhi")
    slots = 2 * parts
    wide = width + EXT
    bf16, f32 = jnp.bfloat16, jnp.float32

    send, pick = call(
        pack_kernel,
        [((slots, wide), bf16), ((rows, slots), bf16)],
        2 * slots * rows * width,
        embeddings,
        inv_temp.reshape(1, rows),
        cluster.reshape(1, rows),
    )
    query = spread(send, parts)

    pairs = [(0, 1), (1, 0)]
    far = lax.ppermute(query, "xlo", pairs)
    near_keys = lax.all_gather(query, "core", axis=0, tiled=True)
    core = lax.axis_index("core").astype(jnp.int32).reshape(1)
    work = 4 * slots * 2 * slots * width
    mass, near = call(
        first_kernel, [((slots, EXT), f32), ((slots, width), f32)], work, core, query, near_keys, scalars=1
    )
    far_keys = lax.all_gather(far, "core", axis=0, tiled=True)
    (result,) = call(second_kernel, [((slots, wide), bf16)], work, query, far_keys, mass, near)

    back = spread(result, parts)
    neigh, dup = call(
        unpack_kernel,
        [((rows, width), bf16), ((1, rows), bf16)],
        2 * slots * rows * wide,
        pick,
        back,
    )
    return neigh, dup.reshape(rows)


def solution(mesh):
    dp, grp = mesh.devices.shape
    z = y = math.isqrt(dp // 2)
    split = Mesh(mesh.devices.reshape(z, y, 2, grp // 2, 2), AXES)
    return jax.shard_map(
        shards,
        mesh=split,
        in_specs=(P(AXES, None), P(AXES), P(AXES, None)),
        out_specs=(P(AXES, None), P(AXES)),
        check_vma=False,
    )
```

```python
import math

import jax
import jax.numpy as jnp
from jax import lax
from jax.experimental import pallas as pl
from jax.experimental.pallas import tpu as pltpu
from jax.sharding import Mesh
from jax.sharding import PartitionSpec as P

NEIGH_SCALE = 8.0
EXT = 128
NT = (((1,), (1,)), ((), ()))

AXES = ("z", "y", "core", "xhi", "xlo")
SPREAD = ("z", "y", "xhi")


def params():
    return pltpu.CompilerParams(vmem_limit_bytes=32 * 1024 * 1024)


def lane_to_row(ext):
    first = (lax.broadcasted_iota(jnp.int32, (16, EXT), 1) == 0).astype(jnp.bfloat16)
    return lax.dot_general(first, ext, NT, preferred_element_type=jnp.float32)[:1]


def pack_kernel(emb_hbm, temp_hbm, cluster_hbm, send_ref, pick_ref, emb_ref, temp_ref, cluster_ref, sems):
    copies = [
        pltpu.make_async_copy(source, target, sems.at[i])
        for i, (source, target) in enumerate(
            ((cluster_hbm, cluster_ref), (temp_hbm, temp_ref), (emb_hbm, emb_ref))
        )
    ]
    for copy in copies:
        copy.start()
    rows, width = emb_ref.shape
    places = send_ref.shape[0]
    slots = pick_ref.shape[1]
    copies[0].wait()
    copies[1].wait()

    cluster_row = cluster_ref[...].astype(jnp.float32)
    row = lax.broadcasted_iota(jnp.int32, (rows, rows), 0)
    col = lax.broadcasted_iota(jnp.int32, (rows, rows), 1)
    cluster_col = jnp.sum(jnp.where(row == col, cluster_row, 0.0), axis=1, keepdims=True)
    same = cluster_row == cluster_col
    rank_row = jnp.sum(jnp.where(same & (row < col), 1.0, 0.0), axis=0, keepdims=True)
    rank_col = jnp.sum(jnp.where(same & (col < row), 1.0, 0.0), axis=1, keepdims=True)
    slot_row = (2.0 * cluster_row + rank_row).astype(jnp.int32)
    slot_col = (2.0 * cluster_col + rank_col).astype(jnp.int32)
    pick = lax.broadcasted_iota(jnp.int32, (rows, slots), 1) == slot_col
    pick_ref[...] = jnp.where(pick, 1.0, 0.0).astype(jnp.bfloat16)

    place = lax.broadcasted_iota(jnp.int32, (places, rows), 0)
    put = 2 * (place >> 2) + (place & 1) == slot_row
    temp = jnp.sum(jnp.where(put, temp_ref[...].astype(jnp.float32), 0.0), axis=1, keepdims=True)
    send_ref[:, width:] = jnp.broadcast_to(temp, (places, EXT)).astype(jnp.bfloat16)

    copies[2].wait()
    values = emb_ref[...].astype(jnp.float32)
    square_mean = jnp.mean(values * values, axis=1, keepdims=True)
    unit = (values * lax.rsqrt(square_mean + 1e-06) * (1.0 / math.sqrt(width))).astype(jnp.bfloat16)
    placed = jnp.dot(
        jnp.where(put, 1.0, 0.0).astype(jnp.bfloat16), unit, preferred_element_type=jnp.float32
    )
    send_ref[:, :width] = placed.astype(jnp.bfloat16)


def weigh(query, key_ref, skipped):
    width = key_ref.shape[1] - EXT
    unit = key_ref[:, :width]
    cosine = lax.dot_general(query[:, :width], unit, NT, preferred_element_type=jnp.float32)
    key_temp = lane_to_row(key_ref[:, width:])
    query_temp = query[:, width : width + 1].astype(jnp.float32)
    weight = jnp.exp((cosine - 1.0) * ((query_temp + key_temp) * 0.5))
    allowed = key_temp > 0.0
    if skipped is not None:
        allowed = allowed & ~skipped
    weight = jnp.where(allowed, weight, 0.0)
    near = jnp.dot(weight.astype(jnp.bfloat16), unit, preferred_element_type=jnp.float32)
    return jnp.sum(weight, axis=1, keepdims=True), near


def first_kernel(xlo_ref, mine_ref, query_ref, mass_ref, near_ref):
    shape = (query_ref.shape[0], mine_ref.shape[0])
    index = lax.broadcasted_iota(jnp.int32, shape, 0)
    place = 4 * (index >> 1) + (index & 1) + 2 * xlo_ref[0]
    own = lax.broadcasted_iota(jnp.int32, shape, 1) == place
    query = jnp.dot(
        jnp.where(own, 1.0, 0.0).astype(jnp.bfloat16),
        mine_ref[...],
        preferred_element_type=jnp.float32,
    ).astype(jnp.bfloat16)
    query_ref[...] = query
    mass, near = weigh(query, mine_ref, own)
    mass_ref[...] = jnp.broadcast_to(mass, mass_ref.shape)
    near_ref[...] = near


def second_kernel(query_ref, key_ref, mass_ref, near_ref, out_ref):
    width = near_ref.shape[1]
    mass, near = weigh(query_ref[...], key_ref, None)
    mass = mass + mass_ref[:, :1]
    near = near + near_ref[...]
    neigh = NEIGH_SCALE * math.sqrt(width) * near / (1.0 + mass)
    out_ref[:, :width] = neigh.astype(jnp.bfloat16)
    out_ref[:, width:] = jnp.broadcast_to(mass, (mass.shape[0], EXT)).astype(jnp.bfloat16)


def unpack_kernel(pick_ref, back_ref, neigh_ref, mass_ref):
    width = neigh_ref.shape[1]
    rows = jnp.dot(pick_ref[...], back_ref[...], preferred_element_type=jnp.float32)
    rows = rows.astype(jnp.bfloat16)
    neigh_ref[...] = rows[:, :width]
    mass_ref[...] = lane_to_row(rows[:, width:]).astype(jnp.bfloat16)


def call(kernel, outs, flops, *args, spaces=None, scratch=()):
    shapes = [jax.ShapeDtypeStruct(shape, dtype) for shape, dtype in outs]
    spaces = spaces or [pltpu.VMEM] * len(args)
    moved = sum(a.size * a.dtype.itemsize for a in args)
    moved += sum(math.prod(s.shape) * s.dtype.itemsize for s in shapes)
    return pl.pallas_call(
        kernel,
        out_shape=shapes,
        in_specs=[pl.BlockSpec(memory_space=space) for space in spaces],
        out_specs=[pl.BlockSpec(memory_space=pltpu.VMEM)] * len(shapes),
        scratch_shapes=scratch,
        compiler_params=params(),
        cost_estimate=pl.CostEstimate(flops=flops, bytes_accessed=moved, transcendentals=0),
    )(*args)


def exchange(slots, axes):
    count, wide = slots.shape
    moved = lax.all_to_all(
        slots.reshape(count // 2, 2, wide), axes, split_axis=0, concat_axis=0, tiled=True
    )
    return moved.reshape(count, wide)


def shards(embeddings, inv_temp, cluster):
    rows, width = embeddings.shape
    slots = 2 * math.prod(lax.axis_size(axis) for axis in SPREAD)
    places = 2 * slots
    wide = width + EXT
    bf16, f32, i32 = jnp.bfloat16, jnp.float32, jnp.int32

    send, pick = call(
        pack_kernel,
        [((places, wide), bf16), ((rows, slots), bf16)],
        2 * places * rows * width,
        embeddings,
        inv_temp.reshape(1, rows),
        cluster.reshape(1, rows),
        spaces=[pltpu.HBM] * 3,
        scratch=[
            pltpu.VMEM((rows, width), bf16),
            pltpu.VMEM((1, rows), bf16),
            pltpu.VMEM((1, rows), i32),
            pltpu.SemaphoreType.DMA((3,)),
        ],
    )
    mine = exchange(send, SPREAD + ("xlo",))
    other = lax.ppermute(mine, "core", [(0, 1), (1, 0)])
    xlo = lax.axis_index("xlo").astype(i32).reshape(1)
    work = 4 * slots * places * width
    query, mass, near = call(
        first_kernel,
        [((slots, wide), bf16), ((slots, EXT), f32), ((slots, width), f32)],
        work,
        xlo,
        mine,
        spaces=[pltpu.SMEM, pltpu.VMEM],
    )
    (result,) = call(second_kernel, [((slots, wide), bf16)], work, query, other, mass, near)
    back = exchange(result, SPREAD)
    neigh, dup = call(
        unpack_kernel,
        [((rows, width), bf16), ((1, rows), bf16)],
        2 * slots * rows * wide,
        pick,
        back,
    )
    return neigh, dup.reshape(rows)


def solution(mesh):
    dp, grp = mesh.devices.shape
    z = y = math.isqrt(dp // 2)
    split = Mesh(mesh.devices.reshape(z, y, 2, grp // 2, 2), AXES)
    return jax.shard_map(
        shards,
        mesh=split,
        in_specs=(P(AXES, None), P(AXES), P(AXES, None)),
        out_specs=(P(AXES, None), P(AXES)),
        check_vma=False,
    )
```

```python
import functools
import math

import jax
import jax.numpy as jnp
import numpy as np
from jax import lax
from jax.experimental import pallas as pl
from jax.experimental.pallas import tpu as pltpu
from jax.sharding import Mesh
from jax.sharding import PartitionSpec as P

NEIGH_SCALE = 8.0
EXT = 128
NT = (((1,), (1,)), ((), ()))

AXES = ("z", "y", "core", "x")


class Layout:
    def __init__(self, dp, grp):
        side = math.isqrt(dp // 2)
        ids = np.arange(dp * grp).reshape(side, side, 2, grp)
        half = [[0, 1], [3, 2]]
        order = [((a + b) % side, a, h) for h in range(2) for b in range(side) for a in range(side)]
        self.spread = [
            [int(ids[z, y, core, half[h][s]]) for z, y, h in order] for core in range(2) for s in range(2)
        ]
        self.pairs = [(x, x ^ 1) for x in range(grp)]
        self.shape = ids.shape


def params():
    return pltpu.CompilerParams(vmem_limit_bytes=32 * 1024 * 1024)


def lane_to_row(ext):
    first = (lax.broadcasted_iota(jnp.int32, (16, EXT), 1) == 0).astype(jnp.bfloat16)
    return lax.dot_general(first, ext, NT, preferred_element_type=jnp.float32)[:1]


def pack_kernel(emb_ref, temp_ref, cluster_ref, send_ref, pick_ref):
    rows, width = emb_ref.shape
    slots = send_ref.shape[0]
    values = emb_ref[...].astype(jnp.float32)
    square_mean = jnp.mean(values * values, axis=1, keepdims=True)
    unit = (values * lax.rsqrt(square_mean + 1e-06) * (1.0 / math.sqrt(width))).astype(jnp.bfloat16)

    cluster_row = cluster_ref[...].astype(jnp.float32)
    row = lax.broadcasted_iota(jnp.int32, (rows, rows), 0)
    col = lax.broadcasted_iota(jnp.int32, (rows, rows), 1)
    cluster_col = jnp.sum(jnp.where(row == col, cluster_row, 0.0), axis=1, keepdims=True)
    same = cluster_row == cluster_col
    rank_row = jnp.sum(jnp.where(same & (row < col), 1.0, 0.0), axis=0, keepdims=True)
    rank_col = jnp.sum(jnp.where(same & (col < row), 1.0, 0.0), axis=1, keepdims=True)
    slot_row = (2.0 * cluster_row + rank_row).astype(jnp.int32)
    slot_col = (2.0 * cluster_col + rank_col).astype(jnp.int32)

    put = lax.broadcasted_iota(jnp.int32, (slots, rows), 0) == slot_row
    placed = jnp.dot(
        jnp.where(put, 1.0, 0.0).astype(jnp.bfloat16), unit, preferred_element_type=jnp.float32
    )
    temp = jnp.sum(jnp.where(put, temp_ref[...].astype(jnp.float32), 0.0), axis=1, keepdims=True)
    send_ref[:, :width] = placed.astype(jnp.bfloat16)
    send_ref[:, width:] = jnp.broadcast_to(temp, (slots, EXT)).astype(jnp.bfloat16)
    pick = lax.broadcasted_iota(jnp.int32, (rows, slots), 1) == slot_col
    pick_ref[...] = jnp.where(pick, 1.0, 0.0).astype(jnp.bfloat16)


def weigh(query_ref, key_ref, own_start):
    width = query_ref.shape[1] - EXT
    unit = key_ref[:, :width]
    cosine = lax.dot_general(
        query_ref[:, :width], unit, NT, preferred_element_type=jnp.float32
    )
    key_temp = lane_to_row(key_ref[:, width:])
    query_temp = query_ref[:, width : width + 1].astype(jnp.float32)
    weight = jnp.exp((cosine - 1.0) * ((query_temp + key_temp) * 0.5))
    allowed = key_temp > 0.0
    if own_start is not None:
        query_index = lax.broadcasted_iota(jnp.int32, cosine.shape, 0) + own_start
        allowed = allowed & (query_index != lax.broadcasted_iota(jnp.int32, cosine.shape, 1))
    weight = jnp.where(allowed, weight, 0.0)
    near = jnp.dot(weight.astype(jnp.bfloat16), unit, preferred_element_type=jnp.float32)
    return jnp.sum(weight, axis=1, keepdims=True), near


def first_kernel(core_ref, query_ref, key_ref, mass_ref, near_ref):
    mass, near = weigh(query_ref, key_ref, core_ref[0] * query_ref.shape[0])
    mass_ref[...] = jnp.broadcast_to(mass, mass_ref.shape)
    near_ref[...] = near


def next_kernel(query_ref, key_ref, mass_in_ref, near_in_ref, mass_ref, near_ref):
    mass, near = weigh(query_ref, key_ref, None)
    mass_ref[...] = jnp.broadcast_to(mass, mass_ref.shape) + mass_in_ref[...]
    near_ref[...] = near + near_in_ref[...]


def last_kernel(query_ref, key_ref, mass_ref, near_ref, out_ref):
    width = near_ref.shape[1]
    mass, near = weigh(query_ref, key_ref, None)
    mass = mass + mass_ref[:, :1]
    near = near + near_ref[...]
    neigh = NEIGH_SCALE * math.sqrt(width) * near / (1.0 + mass)
    out_ref[:, :width] = neigh.astype(jnp.bfloat16)
    out_ref[:, width:] = jnp.broadcast_to(mass, (mass.shape[0], EXT)).astype(jnp.bfloat16)


def unpack_kernel(pick_ref, back_ref, neigh_ref, mass_ref):
    width = neigh_ref.shape[1]
    rows = jnp.dot(pick_ref[...], back_ref[...], preferred_element_type=jnp.float32)
    rows = rows.astype(jnp.bfloat16)
    neigh_ref[...] = rows[:, :width]
    mass_ref[...] = lane_to_row(rows[:, width:]).astype(jnp.bfloat16)


def call(kernel, outs, flops, *args, scalars=0):
    shapes = [jax.ShapeDtypeStruct(shape, dtype) for shape, dtype in outs]
    specs = [pl.BlockSpec(memory_space=pltpu.SMEM)] * scalars
    specs += [pl.BlockSpec(memory_space=pltpu.VMEM)] * (len(args) - scalars)
    moved = sum(a.size * a.dtype.itemsize for a in args)
    moved += sum(math.prod(s.shape) * s.dtype.itemsize for s in shapes)
    return pl.pallas_call(
        kernel,
        out_shape=shapes,
        in_specs=specs,
        out_specs=[pl.BlockSpec(memory_space=pltpu.VMEM)] * len(shapes),
        compiler_params=params(),
        cost_estimate=pl.CostEstimate(flops=flops, bytes_accessed=moved, transcendentals=0),
    )(*args)


def spread(slots, layout):
    count, wide = slots.shape
    moved = lax.all_to_all(
        slots.reshape(count // 2, 2, wide),
        AXES,
        split_axis=0,
        concat_axis=0,
        axis_index_groups=layout.spread,
        tiled=True,
    )
    return moved.reshape(count, wide)


def both_cores(rows):
    return lax.all_gather(rows, "core", axis=0, tiled=True)


def shards(layout, embeddings, inv_temp, cluster):
    rows, width = embeddings.shape
    slots = 2 * len(layout.spread[0])
    wide = width + EXT
    bf16, f32 = jnp.bfloat16, jnp.float32

    send, pick = call(
        pack_kernel,
        [((slots, wide), bf16), ((rows, slots), bf16)],
        2 * slots * rows * width,
        embeddings,
        inv_temp.reshape(1, rows),
        cluster.reshape(1, rows),
    )
    query = spread(send, layout)

    cut = slots * 3 // 4
    far_most = lax.ppermute(query[:cut], "x", layout.pairs)
    far_rest = lax.ppermute(query[cut:], "x", layout.pairs)
    keys = both_cores(query)
    core = lax.axis_index("core").astype(jnp.int32).reshape(1)
    sums = [((slots, EXT), f32), ((slots, width), f32)]
    work = 4 * slots * width
    mass, near = call(first_kernel, sums, 2 * slots * work, core, query, keys, scalars=1)
    keys = both_cores(far_most)
    mass, near = call(next_kernel, sums, 2 * cut * work, query, keys, mass, near)
    keys = both_cores(far_rest)
    (result,) = call(
        last_kernel, [((slots, wide), bf16)], 2 * (slots - cut) * work, query, keys, mass, near
    )

    back = spread(result, layout)
    neigh, dup = call(
        unpack_kernel,
        [((rows, width), bf16), ((1, rows), bf16)],
        2 * slots * rows * wide,
        pick,
        back,
    )
    return neigh, dup.reshape(rows)


def solution(mesh):
    layout = Layout(*mesh.devices.shape)
    split = Mesh(mesh.devices.reshape(layout.shape), AXES)
    return jax.shard_map(
        functools.partial(shards, layout),
        mesh=split,
        in_specs=(P(AXES, None), P(AXES), P(AXES, None)),
        out_specs=(P(AXES, None), P(AXES)),
        check_vma=False,
    )
```

```python
import functools
import math

import jax
import jax.numpy as jnp
import numpy as np
from jax import lax
from jax.experimental import pallas as pl
from jax.experimental.pallas import tpu as pltpu
from jax.sharding import Mesh
from jax.sharding import PartitionSpec as P

NEIGH_SCALE = 8.0
EXT = 128
NT = (((1,), (1,)), ((), ()))

AXES = ("z", "y", "core", "x")


class Layout:
    def __init__(self, dp, grp):
        side = math.isqrt(dp // 2)
        ids = np.arange(dp * grp).reshape(side, side, 2, grp)
        half = [[0, 1], [3, 2]]
        mid = side // 2
        order = [
            ((a + b + mid) % side, (a + mid) % side, h)
            for h in range(2)
            for b in range(side)
            for a in range(side)
        ]
        self.spread = [
            [int(ids[z, y, core, half[h][s]]) for z, y, h in order] for core in range(2) for s in range(2)
        ]
        self.pairs = [(x, x ^ 1) for x in range(grp)]
        self.shape = ids.shape


def params():
    return pltpu.CompilerParams(vmem_limit_bytes=32 * 1024 * 1024)


def lane_to_row(ext):
    first = (lax.broadcasted_iota(jnp.int32, (16, EXT), 1) == 0).astype(jnp.bfloat16)
    return lax.dot_general(first, ext, NT, preferred_element_type=jnp.float32)[:1]


def pack_kernel(emb_ref, temp_ref, cluster_ref, send_ref, pick_ref):
    rows, width = emb_ref.shape
    slots = send_ref.shape[0]
    values = emb_ref[...].astype(jnp.float32)
    square_mean = jnp.mean(values * values, axis=1, keepdims=True)
    unit = (values * lax.rsqrt(square_mean + 1e-06) * (1.0 / math.sqrt(width))).astype(jnp.bfloat16)

    cluster_row = cluster_ref[...].astype(jnp.float32)
    row = lax.broadcasted_iota(jnp.int32, (rows, rows), 0)
    col = lax.broadcasted_iota(jnp.int32, (rows, rows), 1)
    cluster_col = jnp.sum(jnp.where(row == col, cluster_row, 0.0), axis=1, keepdims=True)
    same = cluster_row == cluster_col
    rank_row = jnp.sum(jnp.where(same & (row < col), 1.0, 0.0), axis=0, keepdims=True)
    rank_col = jnp.sum(jnp.where(same & (col < row), 1.0, 0.0), axis=1, keepdims=True)
    slot_row = (2.0 * cluster_row + rank_row).astype(jnp.int32)
    slot_col = (2.0 * cluster_col + rank_col).astype(jnp.int32)

    put = lax.broadcasted_iota(jnp.int32, (slots, rows), 0) == slot_row
    placed = jnp.dot(
        jnp.where(put, 1.0, 0.0).astype(jnp.bfloat16), unit, preferred_element_type=jnp.float32
    )
    temp = jnp.sum(jnp.where(put, temp_ref[...].astype(jnp.float32), 0.0), axis=1, keepdims=True)
    send_ref[:, :width] = placed.astype(jnp.bfloat16)
    send_ref[:, width:] = jnp.broadcast_to(temp, (slots, EXT)).astype(jnp.bfloat16)
    pick = lax.broadcasted_iota(jnp.int32, (rows, slots), 1) == slot_col
    pick_ref[...] = jnp.where(pick, 1.0, 0.0).astype(jnp.bfloat16)


def weigh(query_ref, key_ref, own_start):
    width = query_ref.shape[1] - EXT
    unit = key_ref[:, :width]
    cosine = lax.dot_general(
        query_ref[:, :width], unit, NT, preferred_element_type=jnp.float32
    )
    key_temp = lane_to_row(key_ref[:, width:])
    query_temp = query_ref[:, width : width + 1].astype(jnp.float32)
    weight = jnp.exp((cosine - 1.0) * ((query_temp + key_temp) * 0.5))
    allowed = key_temp > 0.0
    if own_start is not None:
        query_index = lax.broadcasted_iota(jnp.int32, cosine.shape, 0) + own_start
        allowed = allowed & (query_index != lax.broadcasted_iota(jnp.int32, cosine.shape, 1))
    weight = jnp.where(allowed, weight, 0.0)
    near = jnp.dot(weight.astype(jnp.bfloat16), unit, preferred_element_type=jnp.float32)
    return jnp.sum(weight, axis=1, keepdims=True), near


def first_kernel(core_ref, query_ref, key_ref, mass_ref, near_ref):
    mass, near = weigh(query_ref, key_ref, core_ref[0] * query_ref.shape[0])
    mass_ref[...] = jnp.broadcast_to(mass, mass_ref.shape)
    near_ref[...] = near


def last_kernel(query_ref, key_ref, mass_ref, near_ref, out_ref):
    width = near_ref.shape[1]
    mass, near = weigh(query_ref, key_ref, None)
    mass = mass + mass_ref[:, :1]
    near = near + near_ref[...]
    neigh = NEIGH_SCALE * math.sqrt(width) * near / (1.0 + mass)
    out_ref[:, :width] = neigh.astype(jnp.bfloat16)
    out_ref[:, width:] = jnp.broadcast_to(mass, (mass.shape[0], EXT)).astype(jnp.bfloat16)


def unpack_kernel(pick_ref, back_ref, neigh_ref, mass_ref):
    width = neigh_ref.shape[1]
    rows = jnp.dot(pick_ref[...], back_ref[...], preferred_element_type=jnp.float32)
    rows = rows.astype(jnp.bfloat16)
    neigh_ref[...] = rows[:, :width]
    mass_ref[...] = lane_to_row(rows[:, width:]).astype(jnp.bfloat16)


def call(kernel, outs, flops, *args, scalars=0):
    shapes = [jax.ShapeDtypeStruct(shape, dtype) for shape, dtype in outs]
    specs = [pl.BlockSpec(memory_space=pltpu.SMEM)] * scalars
    specs += [pl.BlockSpec(memory_space=pltpu.VMEM)] * (len(args) - scalars)
    moved = sum(a.size * a.dtype.itemsize for a in args)
    moved += sum(math.prod(s.shape) * s.dtype.itemsize for s in shapes)
    return pl.pallas_call(
        kernel,
        out_shape=shapes,
        in_specs=specs,
        out_specs=[pl.BlockSpec(memory_space=pltpu.VMEM)] * len(shapes),
        compiler_params=params(),
        cost_estimate=pl.CostEstimate(flops=flops, bytes_accessed=moved, transcendentals=0),
    )(*args)


def spread(slots, layout):
    count, wide = slots.shape
    moved = lax.all_to_all(
        slots.reshape(count // 2, 2, wide),
        AXES,
        split_axis=0,
        concat_axis=0,
        axis_index_groups=layout.spread,
        tiled=True,
    )
    return moved.reshape(count, wide)


def both_cores(rows):
    return lax.all_gather(rows, "core", axis=0, tiled=True)


def shards(layout, embeddings, inv_temp, cluster):
    rows, width = embeddings.shape
    slots = 2 * len(layout.spread[0])
    wide = width + EXT
    bf16, f32 = jnp.bfloat16, jnp.float32

    send, pick = call(
        pack_kernel,
        [((slots, wide), bf16), ((rows, slots), bf16)],
        2 * slots * rows * width,
        embeddings,
        inv_temp.reshape(1, rows),
        cluster.reshape(1, rows),
    )
    query = spread(send, layout)

    far = lax.ppermute(query, "x", layout.pairs)
    keys = both_cores(query)
    core = lax.axis_index("core").astype(jnp.int32).reshape(1)
    sums = [((slots, EXT), f32), ((slots, width), f32)]
    work = 4 * slots * width
    mass, near = call(first_kernel, sums, 2 * slots * work, core, query, keys, scalars=1)
    keys = both_cores(far)
    (result,) = call(last_kernel, [((slots, wide), bf16)], 2 * slots * work, query, keys, mass, near)

    back = spread(result, layout)
    neigh, dup = call(
        unpack_kernel,
        [((rows, width), bf16), ((1, rows), bf16)],
        2 * slots * rows * wide,
        pick,
        back,
    )
    return neigh, dup.reshape(rows)


def solution(mesh):
    layout = Layout(*mesh.devices.shape)
    split = Mesh(mesh.devices.reshape(layout.shape), AXES)
    return jax.shard_map(
        functools.partial(shards, layout),
        mesh=split,
        in_specs=(P(AXES, None), P(AXES), P(AXES, None)),
        out_specs=(P(AXES, None), P(AXES)),
        check_vma=False,
    )
```

```python
import functools
import math

import jax
import jax.numpy as jnp
import numpy as np
from jax import lax
from jax.experimental import pallas as pl
from jax.experimental.pallas import tpu as pltpu
from jax.sharding import Mesh
from jax.sharding import PartitionSpec as P

NEIGH_SCALE = 8.0
EXT = 128
NT = (((1,), (1,)), ((), ()))

AXES = ("z", "y", "core", "x")


class Layout:
    def __init__(self, dp, grp):
        side = math.isqrt(dp // 2)
        ids = np.arange(dp * grp).reshape(side, side, 2, grp)
        half = [[0, 1], [3, 2]]
        mid = side // 2
        steps = sorted(range(side), key=lambda step: (min(step, side - step), step))
        order = [
            ((a + b + mid) % side, (a + mid) % side, h) for h in range(2) for b in steps for a in steps
        ]
        start = order.index((side - 1, mid, 0))
        self.count = len(order)
        self.shift = start

        def groups(order):
            return [
                [int(ids[z, y, core, half[h][s]]) for z, y, h in order]
                for core in range(2)
                for s in range(2)
            ]

        self.out = groups(order[start:] + order[:start])
        self.back = groups(order)
        self.pairs = [(x, x ^ 1) for x in range(grp)]
        self.shape = ids.shape


def lane_to_row(ext):
    first = (lax.broadcasted_iota(jnp.int32, (16, EXT), 1) == 0).astype(jnp.bfloat16)
    return lax.dot_general(first, ext, NT, preferred_element_type=jnp.float32)[:1]


def pack_kernel(
    shift, emb_hbm, temp_hbm, cluster_hbm, send_ref, pick_ref, emb_ref, temp_ref, cluster_ref, sems
):
    pairs = ((cluster_hbm, cluster_ref), (temp_hbm, temp_ref), (emb_hbm, emb_ref))
    copies = [pltpu.make_async_copy(*pair, sems.at[i]) for i, pair in enumerate(pairs)]
    for copy in copies:
        copy.start()
    rows, width = emb_ref.shape
    slots = send_ref.shape[0]
    copies[0].wait()
    copies[1].wait()

    cluster_row = cluster_ref[...].astype(jnp.float32)
    row = lax.broadcasted_iota(jnp.int32, (rows, rows), 0)
    col = lax.broadcasted_iota(jnp.int32, (rows, rows), 1)
    cluster_col = jnp.sum(jnp.where(row == col, cluster_row, 0.0), axis=1, keepdims=True)
    same = cluster_row == cluster_col
    rank_row = jnp.sum(jnp.where(same & (row < col), 1.0, 0.0), axis=0, keepdims=True)
    rank_col = jnp.sum(jnp.where(same & (col < row), 1.0, 0.0), axis=1, keepdims=True)
    slot_row = (2.0 * cluster_row + rank_row).astype(jnp.int32)
    slot_col = (2.0 * cluster_col + rank_col).astype(jnp.int32) + 2 * shift
    slot_col = jnp.where(slot_col >= slots, slot_col - slots, slot_col)
    pick = lax.broadcasted_iota(jnp.int32, (rows, slots), 1) == slot_col
    pick_ref[...] = jnp.where(pick, 1.0, 0.0).astype(jnp.bfloat16)

    put = lax.broadcasted_iota(jnp.int32, (slots, rows), 0) == slot_row
    temp = jnp.sum(jnp.where(put, temp_ref[...].astype(jnp.float32), 0.0), axis=1, keepdims=True)
    send_ref[:, width:] = jnp.broadcast_to(temp, (slots, EXT)).astype(jnp.bfloat16)

    copies[2].wait()
    values = emb_ref[...].astype(jnp.float32)
    square_mean = jnp.mean(values * values, axis=1, keepdims=True)
    unit = (values * lax.rsqrt(square_mean + 1e-06) * (1.0 / math.sqrt(width))).astype(jnp.bfloat16)
    placed = jnp.dot(
        jnp.where(put, 1.0, 0.0).astype(jnp.bfloat16), unit, preferred_element_type=jnp.float32
    )
    send_ref[:, :width] = placed.astype(jnp.bfloat16)


def weigh(query_ref, key_ref, own_start):
    width = query_ref.shape[1] - EXT
    unit = key_ref[:, :width]
    cosine = lax.dot_general(
        query_ref[:, :width], unit, NT, preferred_element_type=jnp.float32
    )
    key_temp = lane_to_row(key_ref[:, width:])
    query_temp = query_ref[:, width : width + 1].astype(jnp.float32)
    weight = jnp.exp((cosine - 1.0) * ((query_temp + key_temp) * 0.5))
    allowed = key_temp > 0.0
    if own_start is not None:
        query_index = lax.broadcasted_iota(jnp.int32, cosine.shape, 0) + own_start
        allowed = allowed & (query_index != lax.broadcasted_iota(jnp.int32, cosine.shape, 1))
    weight = jnp.where(allowed, weight, 0.0)
    near = jnp.dot(weight.astype(jnp.bfloat16), unit, preferred_element_type=jnp.float32)
    return jnp.sum(weight, axis=1, keepdims=True), near


def first_kernel(core_ref, query_ref, key_ref, mass_ref, near_ref):
    mass, near = weigh(query_ref, key_ref, core_ref[0] * query_ref.shape[0])
    mass_ref[...] = jnp.broadcast_to(mass, mass_ref.shape)
    near_ref[...] = near


def last_kernel(shift, query_ref, key_ref, mass_ref, near_ref, out_ref):
    slots, width = near_ref.shape
    mass, near = weigh(query_ref, key_ref, None)
    mass = mass + mass_ref[:, :1]
    near = near + near_ref[...]
    neigh = NEIGH_SCALE * math.sqrt(width) * near / (1.0 + mass)
    mass = jnp.broadcast_to(mass, (slots, EXT))
    moved = 2 * shift
    for source, target, count in ((0, moved, slots - moved), (slots - moved, 0, moved)):
        out_ref[target : target + count, :width] = neigh[source : source + count].astype(jnp.bfloat16)
        out_ref[target : target + count, width:] = mass[source : source + count].astype(jnp.bfloat16)


def unpack_kernel(pick_ref, back_ref, neigh_ref, mass_ref):
    width = neigh_ref.shape[1]
    rows = jnp.dot(pick_ref[...], back_ref[...], preferred_element_type=jnp.float32)
    rows = rows.astype(jnp.bfloat16)
    neigh_ref[...] = rows[:, :width]
    mass_ref[...] = lane_to_row(rows[:, width:]).astype(jnp.bfloat16)


def call(kernel, outs, flops, *args, spaces=None, scratch=(), room=32 * 2**20):
    shapes = [jax.ShapeDtypeStruct(shape, dtype) for shape, dtype in outs]
    spaces = spaces or [pltpu.VMEM] * len(args)
    moved = sum(a.size * a.dtype.itemsize for a in args)
    moved += sum(math.prod(s.shape) * s.dtype.itemsize for s in shapes)
    return pl.pallas_call(
        kernel,
        out_shape=shapes,
        in_specs=[pl.BlockSpec(memory_space=space) for space in spaces],
        out_specs=[pl.BlockSpec(memory_space=pltpu.VMEM)] * len(shapes),
        scratch_shapes=scratch,
        compiler_params=pltpu.CompilerParams(vmem_limit_bytes=room),
        cost_estimate=pl.CostEstimate(flops=flops, bytes_accessed=moved, transcendentals=0),
    )(*args)


def exchange(slots, groups):
    count, wide = slots.shape
    moved = lax.all_to_all(
        slots.reshape(count // 2, 2, wide),
        AXES,
        split_axis=0,
        concat_axis=0,
        axis_index_groups=groups,
        tiled=True,
    )
    return moved.reshape(count, wide)


def both_cores(rows):
    return lax.all_gather(rows, "core", axis=0, tiled=True)


def shards(layout, embeddings, inv_temp, cluster):
    rows, width = embeddings.shape
    slots = 2 * layout.count
    wide = width + EXT
    bf16, f32 = jnp.bfloat16, jnp.float32

    send, pick = call(
        functools.partial(pack_kernel, layout.shift),
        [((slots, wide), bf16), ((rows, slots), bf16)],
        2 * slots * rows * width,
        embeddings,
        inv_temp.reshape(1, rows),
        cluster.reshape(1, rows),
        spaces=[pltpu.HBM] * 3,
        scratch=[
            pltpu.VMEM((rows, width), bf16),
            pltpu.VMEM((1, rows), bf16),
            pltpu.VMEM((1, rows), jnp.int32),
            pltpu.SemaphoreType.DMA((3,)),
        ],
        room=60 * 2**20,
    )
    query = exchange(send, layout.out)

    far = lax.ppermute(query, "x", layout.pairs)
    keys = both_cores(query)
    core = lax.axis_index("core").astype(jnp.int32).reshape(1)
    sums = [((slots, EXT), f32), ((slots, width), f32)]
    work = 4 * slots * width
    mass, near = call(
        first_kernel, sums, 2 * slots * work, core, query, keys,
        spaces=[pltpu.SMEM, pltpu.VMEM, pltpu.VMEM],
    )
    keys = both_cores(far)
    (result,) = call(
        functools.partial(last_kernel, layout.shift),
        [((slots, wide), bf16)],
        2 * slots * work,
        query,
        keys,
        mass,
        near,
    )

    back = exchange(result, layout.back)
    neigh, dup = call(
        unpack_kernel,
        [((rows, width), bf16), ((1, rows), bf16)],
        2 * slots * rows * wide,
        pick,
        back,
    )
    return neigh, dup.reshape(rows)


def solution(mesh):
    layout = Layout(*mesh.devices.shape)
    split = Mesh(mesh.devices.reshape(layout.shape), AXES)
    return jax.shard_map(
        functools.partial(shards, layout),
        mesh=split,
        in_specs=(P(AXES, None), P(AXES), P(AXES, None)),
        out_specs=(P(AXES, None), P(AXES)),
        check_vma=False,
    )
```

```python
import functools
import math

import jax
import jax.numpy as jnp
import numpy as np
from jax import lax
from jax.experimental import pallas as pl
from jax.experimental.pallas import tpu as pltpu
from jax.sharding import Mesh
from jax.sharding import PartitionSpec as P

NEIGH_SCALE = 8.0
EXT = 128
NT = (((1,), (1,)), ((), ()))

AXES = ("z", "y", "core", "x")


class Layout:
    def __init__(self, dp, grp):
        side = math.isqrt(dp // 2)
        ids = np.arange(dp * grp).reshape(side, side, 2, grp)
        half = [[0, 3], [1, 2]]
        mid = side // 2
        steps = sorted(range(side), key=lambda step: (min(step, side - step), step))
        order = [
            ((a + b + mid) % side, (a + mid) % side, h) for h in range(2) for b in steps for a in steps
        ]
        start = order.index((side - 1, mid, 0))
        self.count = len(order)
        self.shift = start

        def groups(order):
            return [
                [int(ids[z, y, core, half[h][s]]) for z, y, h in order]
                for core in range(2)
                for s in range(2)
            ]

        self.out = groups(order[start:] + order[:start])
        self.back = groups(order)
        self.pairs = [(x, grp - 1 - x) for x in range(grp)]
        self.shape = ids.shape


def lane_to_row(ext):
    first = (lax.broadcasted_iota(jnp.int32, (16, EXT), 1) == 0).astype(jnp.bfloat16)
    return lax.dot_general(first, ext, NT, preferred_element_type=jnp.float32)[:1]


def pack_kernel(shift, emb_ref, temp_ref, cluster_ref, send_ref, pick_ref):
    rows, width = emb_ref.shape
    slots = send_ref.shape[0]

    cluster_row = cluster_ref[...].astype(jnp.float32)
    row = lax.broadcasted_iota(jnp.int32, (rows, rows), 0)
    col = lax.broadcasted_iota(jnp.int32, (rows, rows), 1)
    cluster_col = jnp.sum(jnp.where(row == col, cluster_row, 0.0), axis=1, keepdims=True)
    same = cluster_row == cluster_col
    rank_row = jnp.sum(jnp.where(same & (row < col), 1.0, 0.0), axis=0, keepdims=True)
    rank_col = jnp.sum(jnp.where(same & (col < row), 1.0, 0.0), axis=1, keepdims=True)
    slot_row = (2.0 * cluster_row + rank_row).astype(jnp.int32)
    slot_col = (2.0 * cluster_col + rank_col).astype(jnp.int32) + 2 * shift
    slot_col = jnp.where(slot_col >= slots, slot_col - slots, slot_col)
    pick = lax.broadcasted_iota(jnp.int32, (rows, slots), 1) == slot_col
    pick_ref[...] = jnp.where(pick, 1.0, 0.0).astype(jnp.bfloat16)

    put = lax.broadcasted_iota(jnp.int32, (slots, rows), 0) == slot_row
    temp = jnp.sum(jnp.where(put, temp_ref[...].astype(jnp.float32), 0.0), axis=1, keepdims=True)
    send_ref[:, width:] = jnp.broadcast_to(temp, (slots, EXT)).astype(jnp.bfloat16)

    values = emb_ref[...].astype(jnp.float32)
    square_mean = jnp.mean(values * values, axis=1, keepdims=True)
    unit = (values * lax.rsqrt(square_mean + 1e-06) * (1.0 / math.sqrt(width))).astype(jnp.bfloat16)
    placed = jnp.dot(
        jnp.where(put, 1.0, 0.0).astype(jnp.bfloat16), unit, preferred_element_type=jnp.float32
    )
    send_ref[:, :width] = placed.astype(jnp.bfloat16)


def weigh(query_ref, key_ref, own_start):
    width = query_ref.shape[1] - EXT
    unit = key_ref[:, :width]
    cosine = lax.dot_general(
        query_ref[:, :width], unit, NT, preferred_element_type=jnp.float32
    )
    key_temp = lane_to_row(key_ref[:, width:])
    query_temp = query_ref[:, width : width + 1].astype(jnp.float32)
    weight = jnp.exp((cosine - 1.0) * ((query_temp + key_temp) * 0.5))
    allowed = key_temp > 0.0
    if own_start is not None:
        query_index = lax.broadcasted_iota(jnp.int32, cosine.shape, 0) + own_start
        allowed = allowed & (query_index != lax.broadcasted_iota(jnp.int32, cosine.shape, 1))
    weight = jnp.where(allowed, weight, 0.0)
    near = jnp.dot(weight.astype(jnp.bfloat16), unit, preferred_element_type=jnp.float32)
    return jnp.sum(weight, axis=1, keepdims=True), near


def first_kernel(core_ref, query_ref, key_ref, mass_ref, near_ref):
    mass, near = weigh(query_ref, key_ref, core_ref[0] * query_ref.shape[0])
    mass_ref[...] = jnp.broadcast_to(mass, mass_ref.shape)
    near_ref[...] = near


def last_kernel(shift, query_ref, key_ref, mass_ref, near_ref, out_ref):
    slots, width = near_ref.shape
    mass, near = weigh(query_ref, key_ref, None)
    mass = mass + mass_ref[:, :1]
    near = near + near_ref[...]
    neigh = NEIGH_SCALE * math.sqrt(width) * near / (1.0 + mass)
    mass = jnp.broadcast_to(mass, (slots, EXT))
    moved = 2 * shift
    for source, target, count in ((0, moved, slots - moved), (slots - moved, 0, moved)):
        out_ref[target : target + count, :width] = neigh[source : source + count].astype(jnp.bfloat16)
        out_ref[target : target + count, width:] = mass[source : source + count].astype(jnp.bfloat16)


def unpack_kernel(pick_ref, back_ref, neigh_ref, mass_ref):
    width = neigh_ref.shape[1]
    rows = jnp.dot(pick_ref[...], back_ref[...], preferred_element_type=jnp.float32)
    rows = rows.astype(jnp.bfloat16)
    neigh_ref[...] = rows[:, :width]
    mass_ref[...] = lane_to_row(rows[:, width:]).astype(jnp.bfloat16)


def call(kernel, outs, flops, *args, spaces=None):
    shapes = [jax.ShapeDtypeStruct(shape, dtype) for shape, dtype in outs]
    spaces = spaces or [pltpu.VMEM] * len(args)
    moved = sum(a.size * a.dtype.itemsize for a in args)
    moved += sum(math.prod(s.shape) * s.dtype.itemsize for s in shapes)
    return pl.pallas_call(
        kernel,
        out_shape=shapes,
        in_specs=[pl.BlockSpec(memory_space=space) for space in spaces],
        out_specs=[pl.BlockSpec(memory_space=pltpu.VMEM)] * len(shapes),
        compiler_params=pltpu.CompilerParams(vmem_limit_bytes=32 * 2**20),
        cost_estimate=pl.CostEstimate(flops=flops, bytes_accessed=moved, transcendentals=0),
    )(*args)


def exchange(slots, groups):
    count, wide = slots.shape
    moved = lax.all_to_all(
        slots.reshape(count // 2, 2, wide),
        AXES,
        split_axis=0,
        concat_axis=0,
        axis_index_groups=groups,
        tiled=True,
    )
    return moved.reshape(count, wide)


def both_cores(rows):
    return lax.all_gather(rows, "core", axis=0, tiled=True)


def shards(layout, embeddings, inv_temp, cluster):
    rows, width = embeddings.shape
    slots = 2 * layout.count
    wide = width + EXT
    bf16, f32 = jnp.bfloat16, jnp.float32

    send, pick = call(
        functools.partial(pack_kernel, layout.shift),
        [((slots, wide), bf16), ((rows, slots), bf16)],
        2 * slots * rows * width,
        embeddings,
        inv_temp.reshape(1, rows),
        cluster.reshape(1, rows),
    )
    query = exchange(send, layout.out)

    far = lax.ppermute(query, "x", layout.pairs)
    keys = both_cores(query)
    core = lax.axis_index("core").astype(jnp.int32).reshape(1)
    sums = [((slots, EXT), f32), ((slots, width), f32)]
    work = 4 * slots * width
    mass, near = call(
        first_kernel, sums, 2 * slots * work, core, query, keys,
        spaces=[pltpu.SMEM, pltpu.VMEM, pltpu.VMEM],
    )
    keys = both_cores(far)
    (result,) = call(
        functools.partial(last_kernel, layout.shift),
        [((slots, wide), bf16)],
        2 * slots * work,
        query,
        keys,
        mass,
        near,
    )

    back = exchange(result, layout.back)
    neigh, dup = call(
        unpack_kernel,
        [((rows, width), bf16), ((1, rows), bf16)],
        2 * slots * rows * wide,
        pick,
        back,
    )
    return neigh, dup.reshape(rows)


def solution(mesh):
    layout = Layout(*mesh.devices.shape)
    split = Mesh(mesh.devices.reshape(layout.shape), AXES)
    return jax.shard_map(
        functools.partial(shards, layout),
        mesh=split,
        in_specs=(P(AXES, None), P(AXES), P(AXES, None)),
        out_specs=(P(AXES, None), P(AXES)),
        check_vma=False,
    )
```

```python
import functools
import math

import jax
import jax.numpy as jnp
import numpy as np
from jax import lax
from jax.experimental import pallas as pl
from jax.experimental.pallas import tpu as pltpu
from jax.sharding import Mesh
from jax.sharding import PartitionSpec as P

NEIGH_SCALE = 8.0
EXT = 128
NT = (((1,), (1,)), ((), ()))

AXES = ("z", "y", "core", "x")


class Layout:
    def __init__(self, dp, grp):
        side = math.isqrt(dp // 2)
        ids = np.arange(dp * grp).reshape(side, side, 2, grp)
        half = [[0, 3], [1, 2]]
        mid = side // 2
        steps = sorted(range(side), key=lambda step: (min(step, side - step), step))
        order = [
            ((a + b + mid) % side, (a + mid) % side, h) for h in range(2) for b in steps for a in steps
        ]
        start = order.index((side - 1, mid, 0))
        self.count = len(order)
        self.shift = start

        def group(order, core, s):
            return [int(ids[z, y, core, half[h][s]]) for z, y, h in order]

        turned = order[start:] + order[:start]
        self.out = [group(turned, core, 0) + group(turned, core, 1) for core in range(2)]
        self.back = [group(order, core, s) for core in range(2) for s in range(2)]
        self.shape = ids.shape


def lane_to_row(ext):
    first = (lax.broadcasted_iota(jnp.int32, (16, EXT), 1) == 0).astype(jnp.bfloat16)
    return lax.dot_general(first, ext, NT, preferred_element_type=jnp.float32)[:1]


def pack_kernel(shift, emb_ref, temp_ref, cluster_ref, send_ref, pick_ref):
    rows, width = emb_ref.shape
    slots = pick_ref.shape[1]

    cluster_row = cluster_ref[...].astype(jnp.float32)
    row = lax.broadcasted_iota(jnp.int32, (rows, rows), 0)
    col = lax.broadcasted_iota(jnp.int32, (rows, rows), 1)
    cluster_col = jnp.sum(jnp.where(row == col, cluster_row, 0.0), axis=1, keepdims=True)
    same = cluster_row == cluster_col
    rank_row = jnp.sum(jnp.where(same & (row < col), 1.0, 0.0), axis=0, keepdims=True)
    rank_col = jnp.sum(jnp.where(same & (col < row), 1.0, 0.0), axis=1, keepdims=True)
    slot_row = (2.0 * cluster_row + rank_row).astype(jnp.int32)
    slot_col = (2.0 * cluster_col + rank_col).astype(jnp.int32) + 2 * shift
    slot_col = jnp.where(slot_col >= slots, slot_col - slots, slot_col)
    pick = lax.broadcasted_iota(jnp.int32, (rows, slots), 1) == slot_col
    pick_ref[...] = jnp.where(pick, 1.0, 0.0).astype(jnp.bfloat16)

    put = lax.broadcasted_iota(jnp.int32, (slots, rows), 0) == slot_row
    temp = jnp.sum(jnp.where(put, temp_ref[...].astype(jnp.float32), 0.0), axis=1, keepdims=True)
    temp = jnp.broadcast_to(temp, (slots, EXT)).astype(jnp.bfloat16)

    values = emb_ref[...].astype(jnp.float32)
    square_mean = jnp.mean(values * values, axis=1, keepdims=True)
    unit = (values * lax.rsqrt(square_mean + 1e-06) * (1.0 / math.sqrt(width))).astype(jnp.bfloat16)
    placed = jnp.dot(
        jnp.where(put, 1.0, 0.0).astype(jnp.bfloat16), unit, preferred_element_type=jnp.float32
    )
    placed = placed.astype(jnp.bfloat16)
    for side in range(2):
        send_ref[side * slots : (side + 1) * slots, :width] = placed
        send_ref[side * slots : (side + 1) * slots, width:] = temp


def weigh(query, key_ref, own_start):
    width = key_ref.shape[1] - EXT
    unit = key_ref[:, :width]
    cosine = lax.dot_general(query[:, :width], unit, NT, preferred_element_type=jnp.float32)
    key_temp = lane_to_row(key_ref[:, width:])
    query_temp = query[:, width : width + 1].astype(jnp.float32)
    weight = jnp.exp((cosine - 1.0) * ((query_temp + key_temp) * 0.5))
    allowed = key_temp > 0.0
    if own_start is not None:
        query_index = lax.broadcasted_iota(jnp.int32, cosine.shape, 0) + own_start
        allowed = allowed & (query_index != lax.broadcasted_iota(jnp.int32, cosine.shape, 1))
    weight = jnp.where(allowed, weight, 0.0)
    near = jnp.dot(weight.astype(jnp.bfloat16), unit, preferred_element_type=jnp.float32)
    return jnp.sum(weight, axis=1, keepdims=True), near


def query_rows(side_ref, mine_ref, slots):
    start = pl.multiple_of(side_ref[0] * slots, slots)
    return start, mine_ref[pl.ds(start, slots), :]


def first_kernel(side_ref, mine_ref, mass_ref, near_ref):
    start, query = query_rows(side_ref, mine_ref, near_ref.shape[0])
    mass, near = weigh(query, mine_ref, start)
    mass_ref[...] = jnp.broadcast_to(mass, mass_ref.shape)
    near_ref[...] = near


def last_kernel(shift, side_ref, mine_ref, key_ref, mass_ref, near_ref, out_ref):
    slots, width = near_ref.shape
    _, query = query_rows(side_ref, mine_ref, slots)
    mass, near = weigh(query, key_ref, None)
    mass = mass + mass_ref[:, :1]
    near = near + near_ref[...]
    neigh = NEIGH_SCALE * math.sqrt(width) * near / (1.0 + mass)
    mass = jnp.broadcast_to(mass, (slots, EXT))
    moved = 2 * shift
    for source, target, count in ((0, moved, slots - moved), (slots - moved, 0, moved)):
        out_ref[target : target + count, :width] = neigh[source : source + count].astype(jnp.bfloat16)
        out_ref[target : target + count, width:] = mass[source : source + count].astype(jnp.bfloat16)


def unpack_kernel(pick_ref, back_ref, neigh_ref, mass_ref):
    width = neigh_ref.shape[1]
    rows = jnp.dot(pick_ref[...], back_ref[...], preferred_element_type=jnp.float32)
    rows = rows.astype(jnp.bfloat16)
    neigh_ref[...] = rows[:, :width]
    mass_ref[...] = lane_to_row(rows[:, width:]).astype(jnp.bfloat16)


def call(kernel, outs, flops, *args, spaces=None):
    shapes = [jax.ShapeDtypeStruct(shape, dtype) for shape, dtype in outs]
    spaces = spaces or [pltpu.VMEM] * len(args)
    moved = sum(a.size * a.dtype.itemsize for a in args)
    moved += sum(math.prod(s.shape) * s.dtype.itemsize for s in shapes)
    return pl.pallas_call(
        kernel,
        out_shape=shapes,
        in_specs=[pl.BlockSpec(memory_space=space) for space in spaces],
        out_specs=[pl.BlockSpec(memory_space=pltpu.VMEM)] * len(shapes),
        compiler_params=pltpu.CompilerParams(vmem_limit_bytes=32 * 2**20),
        cost_estimate=pl.CostEstimate(flops=flops, bytes_accessed=moved, transcendentals=0),
    )(*args)


def exchange(slots, groups):
    count, wide = slots.shape
    moved = lax.all_to_all(
        slots.reshape(count // 2, 2, wide),
        AXES,
        split_axis=0,
        concat_axis=0,
        axis_index_groups=groups,
        tiled=True,
    )
    return moved.reshape(count, wide)


def shards(layout, embeddings, inv_temp, cluster):
    rows, width = embeddings.shape
    slots = 2 * layout.count
    wide = width + EXT
    bf16, f32 = jnp.bfloat16, jnp.float32

    send, pick = call(
        functools.partial(pack_kernel, layout.shift),
        [((2 * slots, wide), bf16), ((rows, slots), bf16)],
        2 * slots * rows * width,
        embeddings,
        inv_temp.reshape(1, rows),
        cluster.reshape(1, rows),
    )
    mine = exchange(send, layout.out)
    other = lax.ppermute(mine, "core", [(0, 1), (1, 0)])
    side = (lax.axis_index("x") // 2).astype(jnp.int32).reshape(1)
    work = 8 * slots * slots * width
    spaces = [pltpu.SMEM] + [pltpu.VMEM] * 4
    mass, near = call(
        first_kernel, [((slots, EXT), f32), ((slots, width), f32)], work, side, mine, spaces=spaces[:2]
    )
    (result,) = call(
        functools.partial(last_kernel, layout.shift),
        [((slots, wide), bf16)],
        work,
        side,
        mine,
        other,
        mass,
        near,
        spaces=spaces,
    )
    back = exchange(result, layout.back)
    neigh, dup = call(
        unpack_kernel,
        [((rows, width), bf16), ((1, rows), bf16)],
        2 * slots * rows * wide,
        pick,
        back,
    )
    return neigh, dup.reshape(rows)


def solution(mesh):
    layout = Layout(*mesh.devices.shape)
    split = Mesh(mesh.devices.reshape(layout.shape), AXES)
    return jax.shard_map(
        functools.partial(shards, layout),
        mesh=split,
        in_specs=(P(AXES, None), P(AXES), P(AXES, None)),
        out_specs=(P(AXES, None), P(AXES)),
        check_vma=False,
    )
```

```python
import functools
import math

import jax
import jax.numpy as jnp
import numpy as np
from jax import lax
from jax.experimental import pallas as pl
from jax.experimental.pallas import tpu as pltpu
from jax.sharding import Mesh
from jax.sharding import PartitionSpec as P

NEIGH_SCALE = 8.0
EXT = 128
NT = (((1,), (1,)), ((), ()))

AXES = ("z", "y", "core", "x")


class Layout:
    def __init__(self, dp, grp):
        side = math.isqrt(dp // 2)
        ids = np.arange(dp * grp).reshape(side, side, 2, grp)
        half = [[0, 3], [1, 2]]
        mid = side // 2
        steps = sorted(range(side), key=lambda step: (min(step, side - step), step))
        order = [
            ((a + b + mid) % side, (a + mid) % side, h) for h in range(2) for b in steps for a in steps
        ]
        start = order.index((side - 1, mid, 0))
        self.count = len(order)
        self.shift = start

        def groups(order):
            return [
                [int(ids[z, y, core, half[h][s]]) for z, y, h in order]
                for core in range(2)
                for s in range(2)
            ]

        self.out = groups(order[start:] + order[:start])
        self.back = groups(order)
        self.pairs = [(x, grp - 1 - x) for x in range(grp)]
        self.shape = ids.shape


def lane_to_row(ext):
    first = (lax.broadcasted_iota(jnp.int32, (16, EXT), 1) == 0).astype(jnp.bfloat16)
    return lax.dot_general(first, ext, NT, preferred_element_type=jnp.float32)[:1]


def pack_kernel(shift, emb_ref, temp_ref, cluster_ref, send_ref, pick_ref):
    rows, width = emb_ref.shape
    slots = send_ref.shape[0]

    cluster_row = cluster_ref[...].astype(jnp.float32)
    row = lax.broadcasted_iota(jnp.int32, (rows, rows), 0)
    col = lax.broadcasted_iota(jnp.int32, (rows, rows), 1)
    cluster_col = jnp.sum(jnp.where(row == col, cluster_row, 0.0), axis=1, keepdims=True)
    same = cluster_row == cluster_col
    rank_row = jnp.sum(jnp.where(same & (row < col), 1.0, 0.0), axis=0, keepdims=True)
    rank_col = jnp.sum(jnp.where(same & (col < row), 1.0, 0.0), axis=1, keepdims=True)
    slot_row = (2.0 * cluster_row + rank_row).astype(jnp.int32)
    slot_col = (2.0 * cluster_col + rank_col).astype(jnp.int32) + 2 * shift
    slot_col = jnp.where(slot_col >= slots, slot_col - slots, slot_col)
    pick = lax.broadcasted_iota(jnp.int32, (rows, slots), 1) == slot_col
    pick_ref[...] = jnp.where(pick, 1.0, 0.0).astype(jnp.bfloat16)

    put = lax.broadcasted_iota(jnp.int32, (slots, rows), 0) == slot_row
    temp = jnp.sum(jnp.where(put, temp_ref[...].astype(jnp.float32), 0.0), axis=1, keepdims=True)
    send_ref[:, width:] = jnp.broadcast_to(temp, (slots, EXT)).astype(jnp.bfloat16)

    values = emb_ref[...].astype(jnp.float32)
    square_mean = jnp.mean(values * values, axis=1, keepdims=True)
    unit = (values * lax.rsqrt(square_mean + 1e-06) * (1.0 / math.sqrt(width))).astype(jnp.bfloat16)
    placed = jnp.dot(
        jnp.where(put, 1.0, 0.0).astype(jnp.bfloat16), unit, preferred_element_type=jnp.float32
    )
    send_ref[:, :width] = placed.astype(jnp.bfloat16)


def weigh(query_ref, unit, key_temp, own_start):
    width = unit.shape[1]
    cosine = lax.dot_general(
        query_ref[:, :width], unit, NT, preferred_element_type=jnp.float32
    )
    query_temp = query_ref[:, width : width + 1].astype(jnp.float32)
    weight = jnp.exp((cosine - 1.0) * ((query_temp + key_temp) * 0.5))
    allowed = key_temp > 0.0
    if own_start is not None:
        query_index = lax.broadcasted_iota(jnp.int32, cosine.shape, 0) + own_start
        allowed = allowed & (query_index != lax.broadcasted_iota(jnp.int32, cosine.shape, 1))
    weight = jnp.where(allowed, weight, 0.0)
    near = jnp.dot(weight.astype(jnp.bfloat16), unit, preferred_element_type=jnp.float32)
    return jnp.sum(weight, axis=1, keepdims=True), near


def first_kernel(core_ref, query_ref, key_ref, mass_ref, near_ref, temp_ref):
    slots, width = near_ref.shape
    temp = lane_to_row(key_ref[:, width:])
    temp_ref[...] = jnp.broadcast_to(temp, temp_ref.shape).astype(jnp.bfloat16)
    mass, near = weigh(query_ref, key_ref[:, :width], temp, core_ref[0] * slots)
    mass_ref[...] = jnp.broadcast_to(mass, mass_ref.shape)
    near_ref[...] = near


def last_kernel(shift, query_ref, unit_ref, temp_ref, mass_ref, near_ref, out_ref):
    slots, width = near_ref.shape
    mass, near = weigh(query_ref, unit_ref[...], temp_ref[:1].astype(jnp.float32), None)
    mass = mass + mass_ref[:, :1]
    near = near + near_ref[...]
    neigh = NEIGH_SCALE * math.sqrt(width) * near / (1.0 + mass)
    mass = jnp.broadcast_to(mass, (slots, EXT))
    moved = 2 * shift
    for source, target, count in ((0, moved, slots - moved), (slots - moved, 0, moved)):
        out_ref[target : target + count, :width] = neigh[source : source + count].astype(jnp.bfloat16)
        out_ref[target : target + count, width:] = mass[source : source + count].astype(jnp.bfloat16)


def unpack_kernel(pick_ref, back_ref, neigh_ref, mass_ref):
    width = neigh_ref.shape[1]
    rows = jnp.dot(pick_ref[...], back_ref[...], preferred_element_type=jnp.float32)
    rows = rows.astype(jnp.bfloat16)
    neigh_ref[...] = rows[:, :width]
    mass_ref[...] = lane_to_row(rows[:, width:]).astype(jnp.bfloat16)


def call(kernel, outs, flops, *args, spaces=None):
    shapes = [jax.ShapeDtypeStruct(shape, dtype) for shape, dtype in outs]
    spaces = spaces or [pltpu.VMEM] * len(args)
    moved = sum(a.size * a.dtype.itemsize for a in args)
    moved += sum(math.prod(s.shape) * s.dtype.itemsize for s in shapes)
    return pl.pallas_call(
        kernel,
        out_shape=shapes,
        in_specs=[pl.BlockSpec(memory_space=space) for space in spaces],
        out_specs=[pl.BlockSpec(memory_space=pltpu.VMEM)] * len(shapes),
        compiler_params=pltpu.CompilerParams(vmem_limit_bytes=32 * 2**20),
        cost_estimate=pl.CostEstimate(flops=flops, bytes_accessed=moved, transcendentals=0),
    )(*args)


def exchange(slots, groups):
    count, wide = slots.shape
    return lax.all_to_all(
        slots.reshape(count // 2, 2, wide),
        AXES,
        split_axis=0,
        concat_axis=0,
        axis_index_groups=groups,
        tiled=True,
    )


def both_cores(rows):
    return lax.all_gather(rows, "core", axis=0, tiled=True)


def shards(layout, embeddings, inv_temp, cluster):
    rows, width = embeddings.shape
    slots = 2 * layout.count
    wide = width + EXT
    bf16, f32 = jnp.bfloat16, jnp.float32

    send, pick = call(
        functools.partial(pack_kernel, layout.shift),
        [((slots, wide), bf16), ((rows, slots), bf16)],
        2 * slots * rows * width,
        embeddings,
        inv_temp.reshape(1, rows),
        cluster.reshape(1, rows),
    )
    mine = exchange(send, layout.out)
    far = lax.ppermute(mine[:, :, :width].reshape(slots, width), "x", layout.pairs)
    query = mine.reshape(slots, wide)
    keys = both_cores(query)
    core = lax.axis_index("core").astype(jnp.int32).reshape(1)
    work = 8 * slots * slots * width
    mass, near, temps = call(
        first_kernel,
        [((slots, EXT), f32), ((slots, width), f32), ((16, 2 * slots), bf16)],
        work,
        core,
        query,
        keys,
        spaces=[pltpu.SMEM, pltpu.VMEM, pltpu.VMEM],
    )
    far_temps = lax.ppermute(temps, "x", layout.pairs)
    far_keys = both_cores(far)
    (result,) = call(
        functools.partial(last_kernel, layout.shift),
        [((slots, wide), bf16)],
        work,
        query,
        far_keys,
        far_temps,
        mass,
        near,
    )

    back = exchange(result, layout.back).reshape(slots, wide)
    neigh, dup = call(
        unpack_kernel,
        [((rows, width), bf16), ((1, rows), bf16)],
        2 * slots * rows * wide,
        pick,
        back,
    )
    return neigh, dup.reshape(rows)


def solution(mesh):
    layout = Layout(*mesh.devices.shape)
    split = Mesh(mesh.devices.reshape(layout.shape), AXES)
    return jax.shard_map(
        functools.partial(shards, layout),
        mesh=split,
        in_specs=(P(AXES, None), P(AXES), P(AXES, None)),
        out_specs=(P(AXES, None), P(AXES)),
        check_vma=False,
    )
```

```python
import functools
import math

import jax
import jax.numpy as jnp
import numpy as np
from jax import lax
from jax.experimental import pallas as pl
from jax.experimental.pallas import tpu as pltpu
from jax.sharding import Mesh
from jax.sharding import PartitionSpec as P

NEIGH_SCALE = 8.0
EXT = 128
NT = (((1,), (1,)), ((), ()))

AXES = ("z", "y", "core", "x")


class Layout:
    def __init__(self, dp, grp):
        side = math.isqrt(dp // 2)
        ids = np.arange(dp * grp).reshape(side, side, 2, grp)
        half = [[1, 2], [0, 3]]
        mid = side // 2
        steps = sorted(range(side), key=lambda step: (min(step, side - step), step))
        order = [
            ((a + b + mid) % side, (a + mid) % side, h) for h in range(2) for b in steps for a in steps
        ]
        start = order.index((side - 1, mid, 0))
        self.count = len(order)
        self.shift = start

        def groups(order):
            return [
                [int(ids[z, y, core, half[h][s]]) for z, y, h in order]
                for core in range(2)
                for s in range(2)
            ]

        self.out = groups(order[start:] + order[:start])
        self.back = groups(order)
        self.pairs = [(x, grp - 1 - x) for x in range(grp)]
        self.shape = ids.shape


def lane_to_row(ext):
    first = (lax.broadcasted_iota(jnp.int32, (16, EXT), 1) == 0).astype(jnp.bfloat16)
    return lax.dot_general(first, ext, NT, preferred_element_type=jnp.float32)[:1]


def place_kernel(shift, temp_ref, cluster_ref, put_ref, temps_ref, pick_ref):
    slots, rows = put_ref.shape
    cluster_row = cluster_ref[...].astype(jnp.float32)
    row = lax.broadcasted_iota(jnp.int32, (rows, rows), 0)
    col = lax.broadcasted_iota(jnp.int32, (rows, rows), 1)
    cluster_col = jnp.sum(jnp.where(row == col, cluster_row, 0.0), axis=1, keepdims=True)
    same = cluster_row == cluster_col
    rank_row = jnp.sum(jnp.where(same & (row < col), 1.0, 0.0), axis=0, keepdims=True)
    rank_col = jnp.sum(jnp.where(same & (col < row), 1.0, 0.0), axis=1, keepdims=True)
    slot_row = (2.0 * cluster_row + rank_row).astype(jnp.int32)
    slot_col = (2.0 * cluster_col + rank_col).astype(jnp.int32) + 2 * shift
    slot_col = jnp.where(slot_col >= slots, slot_col - slots, slot_col)
    pick = lax.broadcasted_iota(jnp.int32, (rows, slots), 1) == slot_col
    pick_ref[...] = jnp.where(pick, 1.0, 0.0).astype(jnp.bfloat16)
    put = lax.broadcasted_iota(jnp.int32, (slots, rows), 0) == slot_row
    put_ref[...] = jnp.where(put, 1.0, 0.0).astype(jnp.bfloat16)
    temp = jnp.sum(jnp.where(put, temp_ref[...].astype(jnp.float32), 0.0), axis=1, keepdims=True)
    temps_ref[...] = jnp.broadcast_to(temp, (slots, EXT)).astype(jnp.bfloat16)


def pack_kernel(emb_ref, put_ref, temps_ref, send_ref):
    width = emb_ref.shape[1]
    values = emb_ref[...].astype(jnp.float32)
    square_mean = jnp.mean(values * values, axis=1, keepdims=True)
    unit = (values * lax.rsqrt(square_mean + 1e-06) * (1.0 / math.sqrt(width))).astype(jnp.bfloat16)
    placed = jnp.dot(put_ref[...], unit, preferred_element_type=jnp.float32)
    send_ref[:, :width] = placed.astype(jnp.bfloat16)
    send_ref[:, width:] = temps_ref[...]


def weigh(query_ref, unit, key_temp, own_start):
    width = unit.shape[1]
    cosine = lax.dot_general(
        query_ref[:, :width], unit, NT, preferred_element_type=jnp.float32
    )
    query_temp = query_ref[:, width : width + 1].astype(jnp.float32)
    weight = jnp.exp((cosine - 1.0) * ((query_temp + key_temp) * 0.5))
    allowed = key_temp > 0.0
    if own_start is not None:
        query_index = lax.broadcasted_iota(jnp.int32, cosine.shape, 0) + own_start
        allowed = allowed & (query_index != lax.broadcasted_iota(jnp.int32, cosine.shape, 1))
    weight = jnp.where(allowed, weight, 0.0)
    near = jnp.dot(weight.astype(jnp.bfloat16), unit, preferred_element_type=jnp.float32)
    return jnp.sum(weight, axis=1, keepdims=True), near


def first_kernel(core_ref, query_ref, key_ref, mass_ref, near_ref, temp_ref):
    slots, width = near_ref.shape
    temp = lane_to_row(key_ref[:, width:])
    temp_ref[...] = jnp.broadcast_to(temp, temp_ref.shape).astype(jnp.bfloat16)
    mass, near = weigh(query_ref, key_ref[:, :width], temp, core_ref[0] * slots)
    mass_ref[...] = jnp.broadcast_to(mass, mass_ref.shape)
    near_ref[...] = near


def last_kernel(shift, query_ref, unit_ref, temp_ref, mass_ref, near_ref, out_ref):
    slots, width = near_ref.shape
    mass, near = weigh(query_ref, unit_ref[...], temp_ref[:1].astype(jnp.float32), None)
    mass = mass + mass_ref[:, :1]
    near = near + near_ref[...]
    neigh = NEIGH_SCALE * math.sqrt(width) * near / (1.0 + mass)
    mass = jnp.broadcast_to(mass, (slots, EXT))
    moved = 2 * shift
    for source, target, count in ((0, moved, slots - moved), (slots - moved, 0, moved)):
        out_ref[target : target + count, :width] = neigh[source : source + count].astype(jnp.bfloat16)
        out_ref[target : target + count, width:] = mass[source : source + count].astype(jnp.bfloat16)


def unpack_kernel(pick_ref, back_ref, neigh_ref, mass_ref):
    width = neigh_ref.shape[1]
    rows = jnp.dot(pick_ref[...], back_ref[...], preferred_element_type=jnp.float32)
    rows = rows.astype(jnp.bfloat16)
    neigh_ref[...] = rows[:, :width]
    mass_ref[...] = lane_to_row(rows[:, width:]).astype(jnp.bfloat16)


def call(kernel, outs, flops, *args, spaces=None):
    shapes = [jax.ShapeDtypeStruct(shape, dtype) for shape, dtype in outs]
    spaces = spaces or [pltpu.VMEM] * len(args)
    moved = sum(a.size * a.dtype.itemsize for a in args)
    moved += sum(math.prod(s.shape) * s.dtype.itemsize for s in shapes)
    return pl.pallas_call(
        kernel,
        out_shape=shapes,
        in_specs=[pl.BlockSpec(memory_space=space) for space in spaces],
        out_specs=[pl.BlockSpec(memory_space=pltpu.VMEM)] * len(shapes),
        compiler_params=pltpu.CompilerParams(vmem_limit_bytes=32 * 2**20),
        cost_estimate=pl.CostEstimate(flops=flops, bytes_accessed=moved, transcendentals=0),
    )(*args)


def exchange(slots, groups):
    count, wide = slots.shape
    return lax.all_to_all(
        slots.reshape(count // 2, 2, wide),
        AXES,
        split_axis=0,
        concat_axis=0,
        axis_index_groups=groups,
        tiled=True,
    )


def both_cores(rows):
    return lax.all_gather(rows, "core", axis=0, tiled=True)


def shards(layout, embeddings, inv_temp, cluster):
    rows, width = embeddings.shape
    slots = 2 * layout.count
    wide = width + EXT
    bf16, f32 = jnp.bfloat16, jnp.float32

    put, temps, pick = call(
        functools.partial(place_kernel, layout.shift),
        [((slots, rows), bf16), ((slots, EXT), bf16), ((rows, slots), bf16)],
        2 * slots * rows * rows * rows,
        inv_temp.reshape(1, rows),
        cluster.reshape(1, rows),
    )
    (send,) = call(
        pack_kernel, [((slots, wide), bf16)], 2 * slots * rows * width, embeddings, put, temps
    )
    mine = exchange(send, layout.out)
    far = lax.ppermute(mine[:, :, :width].reshape(slots, width), "x", layout.pairs)
    query = mine.reshape(slots, wide)
    keys = both_cores(query)
    core = lax.axis_index("core").astype(jnp.int32).reshape(1)
    work = 8 * slots * slots * width
    mass, near, temps = call(
        first_kernel,
        [((slots, EXT), f32), ((slots, width), f32), ((16, 2 * slots), bf16)],
        work,
        core,
        query,
        keys,
        spaces=[pltpu.SMEM, pltpu.VMEM, pltpu.VMEM],
    )
    far_temps = lax.ppermute(temps, "x", layout.pairs)
    far_keys = both_cores(far)
    (result,) = call(
        functools.partial(last_kernel, layout.shift),
        [((slots, wide), bf16)],
        work,
        query,
        far_keys,
        far_temps,
        mass,
        near,
    )

    back = exchange(result, layout.back).reshape(slots, wide)
    neigh, dup = call(
        unpack_kernel,
        [((rows, width), bf16), ((1, rows), bf16)],
        2 * slots * rows * wide,
        pick,
        back,
    )
    return neigh, dup.reshape(rows)


def solution(mesh):
    layout = Layout(*mesh.devices.shape)
    split = Mesh(mesh.devices.reshape(layout.shape), AXES)
    return jax.shard_map(
        functools.partial(shards, layout),
        mesh=split,
        in_specs=(P(AXES, None), P(AXES), P(AXES, None)),
        out_specs=(P(AXES, None), P(AXES)),
        check_vma=False,
    )
```

```python
import functools
import math

import jax
import jax.numpy as jnp
import numpy as np
from jax import lax
from jax.experimental import pallas as pl
from jax.experimental.pallas import tpu as pltpu
from jax.sharding import Mesh
from jax.sharding import PartitionSpec as P

NEIGH_SCALE = 8.0
EXT = 128
NT = (((1,), (1,)), ((), ()))

AXES = ("z", "y", "core", "x")


class Layout:
    def __init__(self, dp, grp):
        side = math.isqrt(dp // 2)
        ids = np.arange(dp * grp).reshape(side, side, 2, grp)
        half = [[0, 3], [1, 2]]
        mid = side // 2
        steps = sorted(range(side), key=lambda step: (min(step, side - step), step))
        order = [
            ((a + b + mid) % side, (a + mid) % side, h) for h in range(2) for b in steps for a in steps
        ]
        start = order.index((side - 1, mid, 0))
        self.count = len(order)
        self.shift = start

        def groups(order):
            return [
                [int(ids[z, y, core, half[h][s]]) for z, y, h in order]
                for core in range(2)
                for s in range(2)
            ]

        self.out = groups(order[start:] + order[:start])
        self.back = groups(order)
        self.pairs = [(x, grp - 1 - x) for x in range(grp)]
        self.shape = ids.shape


def lane_to_row(ext):
    first = (lax.broadcasted_iota(jnp.int32, (16, EXT), 1) == 0).astype(jnp.bfloat16)
    return lax.dot_general(first, ext, NT, preferred_element_type=jnp.float32)[:1]


def pack_kernel(shift, emb_ref, temp_ref, cluster_ref, send_ref, pick_ref):
    rows, width = emb_ref.shape
    slots = send_ref.shape[0]

    cluster_row = cluster_ref[...].astype(jnp.float32)
    row = lax.broadcasted_iota(jnp.int32, (rows, rows), 0)
    col = lax.broadcasted_iota(jnp.int32, (rows, rows), 1)
    cluster_col = jnp.sum(jnp.where(row == col, cluster_row, 0.0), axis=1, keepdims=True)
    same = cluster_row == cluster_col
    rank_row = jnp.sum(jnp.where(same & (row < col), 1.0, 0.0), axis=0, keepdims=True)
    rank_col = jnp.sum(jnp.where(same & (col < row), 1.0, 0.0), axis=1, keepdims=True)
    slot_row = (2.0 * cluster_row + rank_row).astype(jnp.int32)
    slot_col = (2.0 * cluster_col + rank_col).astype(jnp.int32) + 2 * shift
    slot_col = jnp.where(slot_col >= slots, slot_col - slots, slot_col)
    pick = lax.broadcasted_iota(jnp.int32, (rows, slots), 1) == slot_col
    pick_ref[...] = jnp.where(pick, 1.0, 0.0).astype(jnp.bfloat16)

    put = lax.broadcasted_iota(jnp.int32, (slots, rows), 0) == slot_row
    temp = jnp.sum(jnp.where(put, temp_ref[...].astype(jnp.float32), 0.0), axis=1, keepdims=True)
    send_ref[:, width:] = jnp.broadcast_to(temp, (slots, EXT)).astype(jnp.bfloat16)

    values = emb_ref[...].astype(jnp.float32)
    square_mean = jnp.mean(values * values, axis=1, keepdims=True)
    unit = (values * lax.rsqrt(square_mean + 1e-06) * (1.0 / math.sqrt(width))).astype(jnp.bfloat16)
    placed = jnp.dot(
        jnp.where(put, 1.0, 0.0).astype(jnp.bfloat16), unit, preferred_element_type=jnp.float32
    )
    send_ref[:, :width] = placed.astype(jnp.bfloat16)


def weigh(query_ref, unit, key_temp, own_start):
    width = unit.shape[1]
    cosine = lax.dot_general(
        query_ref[:, :width], unit, NT, preferred_element_type=jnp.float32
    )
    query_temp = query_ref[:, width : width + 1].astype(jnp.float32)
    weight = jnp.exp((cosine - 1.0) * ((query_temp + key_temp) * 0.5))
    allowed = key_temp > 0.0
    if own_start is not None:
        query_index = lax.broadcasted_iota(jnp.int32, cosine.shape, 0) + own_start
        allowed = allowed & (query_index != lax.broadcasted_iota(jnp.int32, cosine.shape, 1))
    weight = jnp.where(allowed, weight, 0.0)
    near = jnp.dot(weight.astype(jnp.bfloat16), unit, preferred_element_type=jnp.float32)
    return jnp.sum(weight, axis=1, keepdims=True), near


def first_kernel(core_ref, query_ref, key_ref, mass_ref, near_ref, temp_ref):
    slots, width = near_ref.shape
    temp = lane_to_row(key_ref[:, width:])
    temp_ref[...] = jnp.broadcast_to(temp, temp_ref.shape)
    mass, near = weigh(query_ref, key_ref[:, :width], temp, core_ref[0] * slots)
    mass_ref[...] = jnp.broadcast_to(mass, mass_ref.shape)
    near_ref[...] = near


def last_kernel(shift, query_ref, unit_ref, temp_ref, mass_ref, near_ref, out_ref):
    slots, width = near_ref.shape
    mass, near = weigh(query_ref, unit_ref[...], temp_ref[:1], None)
    mass = mass + mass_ref[:, :1]
    near = near + near_ref[...]
    neigh = NEIGH_SCALE * math.sqrt(width) * near / (1.0 + mass)
    mass = jnp.broadcast_to(mass, (slots, EXT))
    moved = 2 * shift
    for source, target, count in ((0, moved, slots - moved), (slots - moved, 0, moved)):
        out_ref[target : target + count, :width] = neigh[source : source + count].astype(jnp.bfloat16)
        out_ref[target : target + count, width:] = mass[source : source + count].astype(jnp.bfloat16)


def unpack_kernel(pick_ref, back_ref, neigh_ref, mass_ref):
    width = neigh_ref.shape[1]
    rows = jnp.dot(pick_ref[...], back_ref[...], preferred_element_type=jnp.float32)
    rows = rows.astype(jnp.bfloat16)
    neigh_ref[...] = rows[:, :width]
    mass_ref[...] = lane_to_row(rows[:, width:]).astype(jnp.bfloat16)


def call(kernel, outs, flops, *args, spaces=None):
    shapes = [jax.ShapeDtypeStruct(shape, dtype) for shape, dtype in outs]
    spaces = spaces or [pltpu.VMEM] * len(args)
    moved = sum(a.size * a.dtype.itemsize for a in args)
    moved += sum(math.prod(s.shape) * s.dtype.itemsize for s in shapes)
    return pl.pallas_call(
        kernel,
        out_shape=shapes,
        in_specs=[pl.BlockSpec(memory_space=space) for space in spaces],
        out_specs=[pl.BlockSpec(memory_space=pltpu.VMEM)] * len(shapes),
        compiler_params=pltpu.CompilerParams(vmem_limit_bytes=32 * 2**20),
        cost_estimate=pl.CostEstimate(flops=flops, bytes_accessed=moved, transcendentals=0),
    )(*args)


def exchange(slots, groups):
    count, wide = slots.shape
    return lax.all_to_all(
        slots.reshape(count // 2, 2, wide),
        AXES,
        split_axis=0,
        concat_axis=0,
        axis_index_groups=groups,
        tiled=True,
    )


def both_cores(rows):
    return lax.all_gather(rows, "core", axis=0, tiled=True)


def shards(layout, embeddings, inv_temp, cluster):
    rows, width = embeddings.shape
    slots = 2 * layout.count
    wide = width + EXT
    bf16, f32 = jnp.bfloat16, jnp.float32

    send, pick = call(
        functools.partial(pack_kernel, layout.shift),
        [((slots, wide), bf16), ((rows, slots), bf16)],
        2 * slots * rows * width,
        embeddings,
        inv_temp.reshape(1, rows),
        cluster.reshape(1, rows),
    )
    mine = exchange(send, layout.out)
    query = lax.optimization_barrier(mine.reshape(slots, wide))
    far = lax.ppermute(query[:, :width], "x", layout.pairs)
    keys = both_cores(query)
    core = lax.axis_index("core").astype(jnp.int32).reshape(1)
    work = 8 * slots * slots * width
    mass, near, temps = call(
        first_kernel,
        [((slots, EXT), f32), ((slots, width), f32), ((8, 2 * slots), f32)],
        work,
        core,
        query,
        keys,
        spaces=[pltpu.SMEM, pltpu.VMEM, pltpu.VMEM],
    )
    far_temps = lax.ppermute(temps, "x", layout.pairs)
    far_keys = both_cores(far)
    (result,) = call(
        functools.partial(last_kernel, layout.shift),
        [((slots, wide), bf16)],
        work,
        query,
        far_keys,
        far_temps,
        mass,
        near,
    )

    back = exchange(result, layout.back).reshape(slots, wide)
    neigh, dup = call(
        unpack_kernel,
        [((rows, width), bf16), ((1, rows), bf16)],
        2 * slots * rows * wide,
        pick,
        back,
    )
    return neigh, dup.reshape(rows)


def solution(mesh):
    layout = Layout(*mesh.devices.shape)
    split = Mesh(mesh.devices.reshape(layout.shape), AXES)
    return jax.shard_map(
        functools.partial(shards, layout),
        mesh=split,
        in_specs=(P(AXES, None), P(AXES), P(AXES, None)),
        out_specs=(P(AXES, None), P(AXES)),
        check_vma=False,
    )
```

```python
import functools
import math

import jax
import jax.numpy as jnp
import numpy as np
from jax import lax
from jax.experimental import pallas as pl
from jax.experimental.pallas import tpu as pltpu
from jax.sharding import Mesh
from jax.sharding import PartitionSpec as P

NEIGH_SCALE = 8.0
EXT = 128
NT = (((1,), (1,)), ((), ()))

AXES = ("z", "y", "core", "x")


class Layout:
    def __init__(self, dp, grp):
        side = math.isqrt(dp // 2)
        ids = np.arange(dp * grp).reshape(side, side, 2, grp)
        half = [[0, 3], [1, 2]]
        mid = side // 2
        steps = sorted(range(side), key=lambda step: (min(step, side - step), step))
        order = [
            ((a + b + mid) % side, (a + mid) % side, h) for h in range(2) for b in steps for a in steps
        ]
        start = order.index((side - 1, mid, 0))
        self.count = len(order)
        self.shift = start

        def groups(order):
            return [
                [int(ids[z, y, core, half[h][s]]) for z, y, h in order]
                for core in range(2)
                for s in range(2)
            ]

        self.out = groups(order[start:] + order[:start])
        self.back = groups(order)
        self.pairs = [(x, grp - 1 - x) for x in range(grp)]
        self.shape = ids.shape


def lane_to_row(ext):
    first = (lax.broadcasted_iota(jnp.int32, (16, EXT), 1) == 0).astype(jnp.bfloat16)
    return lax.dot_general(first, ext, NT, preferred_element_type=jnp.float32)[:1]


def order_kernel(same_ref, before_ref):
    row = lax.broadcasted_iota(jnp.int32, same_ref.shape, 0)
    col = lax.broadcasted_iota(jnp.int32, same_ref.shape, 1)
    same_ref[...] = jnp.where(row == col, 1.0, 0.0)
    before_ref[...] = jnp.where(row < col, 1.0, 0.0)


def pack_kernel(
    shift, emb_ref, temp_ref, cluster_ref, same_ref, before_ref, send_ref, pick_ref
):
    rows, width = emb_ref.shape
    slots = send_ref.shape[0]

    cluster_row = cluster_ref[...].astype(jnp.float32)
    before = before_ref[...]
    after = 1.0 - before - same_ref[...]
    cluster_col = jnp.sum(same_ref[...] * cluster_row, axis=1, keepdims=True)
    alike = cluster_row == cluster_col
    rank_row = jnp.sum(jnp.where(alike, before, 0.0), axis=0, keepdims=True)
    rank_col = jnp.sum(jnp.where(alike, after, 0.0), axis=1, keepdims=True)
    slot_row = (2.0 * cluster_row + rank_row).astype(jnp.int32)
    slot_col = (2.0 * cluster_col + rank_col).astype(jnp.int32) + 2 * shift
    slot_col = jnp.where(slot_col >= slots, slot_col - slots, slot_col)
    pick = lax.broadcasted_iota(jnp.int32, (rows, slots), 1) == slot_col
    pick_ref[...] = jnp.where(pick, 1.0, 0.0).astype(jnp.bfloat16)

    put = lax.broadcasted_iota(jnp.int32, (slots, rows), 0) == slot_row
    temp = jnp.sum(jnp.where(put, temp_ref[...].astype(jnp.float32), 0.0), axis=1, keepdims=True)
    send_ref[:, width:] = jnp.broadcast_to(temp, (slots, EXT)).astype(jnp.bfloat16)

    values = emb_ref[...].astype(jnp.float32)
    square_mean = jnp.mean(values * values, axis=1, keepdims=True)
    unit = (values * lax.rsqrt(square_mean + 1e-06) * (1.0 / math.sqrt(width))).astype(jnp.bfloat16)
    placed = jnp.dot(
        jnp.where(put, 1.0, 0.0).astype(jnp.bfloat16), unit, preferred_element_type=jnp.float32
    )
    send_ref[:, :width] = placed.astype(jnp.bfloat16)


def weigh(query_ref, unit, key_temp, own_start):
    width = unit.shape[1]
    cosine = lax.dot_general(
        query_ref[:, :width], unit, NT, preferred_element_type=jnp.float32
    )
    query_temp = query_ref[:, width : width + 1].astype(jnp.float32)
    weight = jnp.exp((cosine - 1.0) * ((query_temp + key_temp) * 0.5))
    allowed = key_temp > 0.0
    if own_start is not None:
        query_index = lax.broadcasted_iota(jnp.int32, cosine.shape, 0) + own_start
        allowed = allowed & (query_index != lax.broadcasted_iota(jnp.int32, cosine.shape, 1))
    weight = jnp.where(allowed, weight, 0.0)
    near = jnp.dot(weight.astype(jnp.bfloat16), unit, preferred_element_type=jnp.float32)
    return jnp.sum(weight, axis=1, keepdims=True), near


def first_kernel(core_ref, query_ref, key_ref, mass_ref, near_ref, temp_ref):
    slots, width = near_ref.shape
    temp = lane_to_row(key_ref[:, width:])
    temp_ref[...] = jnp.broadcast_to(temp, temp_ref.shape)
    mass, near = weigh(query_ref, key_ref[:, :width], temp, core_ref[0] * slots)
    mass_ref[...] = jnp.broadcast_to(mass, mass_ref.shape)
    near_ref[...] = near


def last_kernel(shift, query_ref, unit_ref, temp_ref, mass_ref, near_ref, out_ref):
    slots, width = near_ref.shape
    mass, near = weigh(query_ref, unit_ref[...], temp_ref[:1], None)
    mass = mass + mass_ref[:, :1]
    near = near + near_ref[...]
    neigh = NEIGH_SCALE * math.sqrt(width) * near / (1.0 + mass)
    mass = jnp.broadcast_to(mass, (slots, EXT))
    moved = 2 * shift
    for source, target, count in ((0, moved, slots - moved), (slots - moved, 0, moved)):
        out_ref[target : target + count, :width] = neigh[source : source + count].astype(jnp.bfloat16)
        out_ref[target : target + count, width:] = mass[source : source + count].astype(jnp.bfloat16)


def unpack_kernel(pick_ref, back_ref, neigh_ref, mass_ref):
    width = neigh_ref.shape[1]
    rows = jnp.dot(pick_ref[...], back_ref[...], preferred_element_type=jnp.float32)
    rows = rows.astype(jnp.bfloat16)
    neigh_ref[...] = rows[:, :width]
    mass_ref[...] = lane_to_row(rows[:, width:]).astype(jnp.bfloat16)


def call(kernel, outs, flops, *args, spaces=None):
    shapes = [jax.ShapeDtypeStruct(shape, dtype) for shape, dtype in outs]
    spaces = spaces or [pltpu.VMEM] * len(args)
    moved = sum(a.size * a.dtype.itemsize for a in args)
    moved += sum(math.prod(s.shape) * s.dtype.itemsize for s in shapes)
    return pl.pallas_call(
        kernel,
        out_shape=shapes,
        in_specs=[pl.BlockSpec(memory_space=space) for space in spaces],
        out_specs=[pl.BlockSpec(memory_space=pltpu.VMEM)] * len(shapes),
        compiler_params=pltpu.CompilerParams(vmem_limit_bytes=32 * 2**20),
        cost_estimate=pl.CostEstimate(flops=flops, bytes_accessed=moved, transcendentals=0),
    )(*args)


def exchange(slots, groups):
    count, wide = slots.shape
    return lax.all_to_all(
        slots.reshape(count // 2, 2, wide),
        AXES,
        split_axis=0,
        concat_axis=0,
        axis_index_groups=groups,
        tiled=True,
    )


def both_cores(rows):
    return lax.all_gather(rows, "core", axis=0, tiled=True)


def shards(layout, embeddings, inv_temp, cluster):
    rows, width = embeddings.shape
    slots = 2 * layout.count
    wide = width + EXT
    bf16, f32 = jnp.bfloat16, jnp.float32

    same, before = call(order_kernel, [((rows, rows), f32)] * 2, 8 * rows * rows * rows * rows)
    send, pick = call(
        functools.partial(pack_kernel, layout.shift),
        [((slots, wide), bf16), ((rows, slots), bf16)],
        2 * slots * rows * width,
        embeddings,
        inv_temp.reshape(1, rows),
        cluster.reshape(1, rows),
        same,
        before,
    )
    mine = exchange(send, layout.out)
    query = lax.optimization_barrier(mine.reshape(slots, wide))
    far = lax.ppermute(query[:, :width], "x", layout.pairs)
    keys = both_cores(query)
    core = lax.axis_index("core").astype(jnp.int32).reshape(1)
    work = 8 * slots * slots * width
    mass, near, temps = call(
        first_kernel,
        [((slots, EXT), f32), ((slots, width), f32), ((8, 2 * slots), f32)],
        work,
        core,
        query,
        keys,
        spaces=[pltpu.SMEM, pltpu.VMEM, pltpu.VMEM],
    )
    far_temps = lax.ppermute(temps, "x", layout.pairs)
    far_keys = both_cores(far)
    (result,) = call(
        functools.partial(last_kernel, layout.shift),
        [((slots, wide), bf16)],
        work,
        query,
        far_keys,
        far_temps,
        mass,
        near,
    )

    back = exchange(result, layout.back).reshape(slots, wide)
    neigh, dup = call(
        unpack_kernel,
        [((rows, width), bf16), ((1, rows), bf16)],
        2 * slots * rows * wide,
        pick,
        back,
    )
    return neigh, dup.reshape(rows)


def solution(mesh):
    layout = Layout(*mesh.devices.shape)
    split = Mesh(mesh.devices.reshape(layout.shape), AXES)
    return jax.shard_map(
        functools.partial(shards, layout),
        mesh=split,
        in_specs=(P(AXES, None), P(AXES), P(AXES, None)),
        out_specs=(P(AXES, None), P(AXES)),
        check_vma=False,
    )
```

```python
import functools
import math

import jax
import jax.numpy as jnp
import numpy as np
from jax import lax
from jax.experimental import pallas as pl
from jax.experimental.pallas import tpu as pltpu
from jax.sharding import Mesh
from jax.sharding import PartitionSpec as P

NEIGH_SCALE = 8.0
EXT = 128
NT = (((1,), (1,)), ((), ()))

AXES = ("z", "y", "core", "x")


class Layout:
    def __init__(self, dp, grp):
        side = math.isqrt(dp // 2)
        ids = np.arange(dp * grp).reshape(side, side, 2, grp)
        half = [[0, 3], [1, 2]]
        mid = side // 2
        steps = sorted(range(side), key=lambda step: (min(step, side - step), step))
        order = [
            ((a + b + mid) % side, (a + mid) % side, h) for h in range(2) for b in steps for a in steps
        ]
        first_out = order.index((side - 1, mid + 1, 0))
        first_back = order.index((mid, mid + 1, 0))
        self.count = len(order)
        self.shift = (first_out - first_back) % self.count

        def groups(start):
            return [
                [int(ids[z, y, core, half[h][s]]) for z, y, h in order[start:] + order[:start]]
                for core in range(2)
                for s in range(2)
            ]

        self.out = groups(first_out)
        self.back = groups(first_back)
        self.pairs = [(x, grp - 1 - x) for x in range(grp)]
        self.shape = ids.shape


def lane_to_row(ext):
    first = (lax.broadcasted_iota(jnp.int32, (16, EXT), 1) == 0).astype(jnp.bfloat16)
    return lax.dot_general(first, ext, NT, preferred_element_type=jnp.float32)[:1]


def order_kernel(same_ref, before_ref):
    row = lax.broadcasted_iota(jnp.int32, same_ref.shape, 0)
    col = lax.broadcasted_iota(jnp.int32, same_ref.shape, 1)
    same_ref[...] = jnp.where(row == col, 1.0, 0.0)
    before_ref[...] = jnp.where(row < col, 1.0, 0.0)


def pack_kernel(
    shift, emb_ref, temp_ref, cluster_ref, same_ref, before_ref, send_ref, pick_ref
):
    rows, width = emb_ref.shape
    slots = send_ref.shape[0]

    cluster_row = cluster_ref[...].astype(jnp.float32)
    before = before_ref[...]
    after = 1.0 - before - same_ref[...]
    cluster_col = jnp.sum(same_ref[...] * cluster_row, axis=1, keepdims=True)
    alike = cluster_row == cluster_col
    rank_row = jnp.sum(jnp.where(alike, before, 0.0), axis=0, keepdims=True)
    rank_col = jnp.sum(jnp.where(alike, after, 0.0), axis=1, keepdims=True)
    slot_row = (2.0 * cluster_row + rank_row).astype(jnp.int32)
    slot_col = (2.0 * cluster_col + rank_col).astype(jnp.int32) + 2 * shift
    slot_col = jnp.where(slot_col >= slots, slot_col - slots, slot_col)
    pick = lax.broadcasted_iota(jnp.int32, (rows, slots), 1) == slot_col
    pick_ref[...] = jnp.where(pick, 1.0, 0.0).astype(jnp.bfloat16)

    put = lax.broadcasted_iota(jnp.int32, (slots, rows), 0) == slot_row
    temp = jnp.sum(jnp.where(put, temp_ref[...].astype(jnp.float32), 0.0), axis=1, keepdims=True)
    send_ref[:, width:] = jnp.broadcast_to(temp, (slots, EXT)).astype(jnp.bfloat16)

    values = emb_ref[...].astype(jnp.float32)
    square_mean = jnp.mean(values * values, axis=1, keepdims=True)
    unit = (values * lax.rsqrt(square_mean + 1e-06) * (1.0 / math.sqrt(width))).astype(jnp.bfloat16)
    placed = jnp.dot(
        jnp.where(put, 1.0, 0.0).astype(jnp.bfloat16), unit, preferred_element_type=jnp.float32
    )
    send_ref[:, :width] = placed.astype(jnp.bfloat16)


def weigh(query_ref, unit, key_temp, own_start):
    width = unit.shape[1]
    cosine = lax.dot_general(
        query_ref[:, :width], unit, NT, preferred_element_type=jnp.float32
    )
    query_temp = query_ref[:, width : width + 1].astype(jnp.float32)
    weight = jnp.exp((cosine - 1.0) * ((query_temp + key_temp) * 0.5))
    allowed = key_temp > 0.0
    if own_start is not None:
        query_index = lax.broadcasted_iota(jnp.int32, cosine.shape, 0) + own_start
        allowed = allowed & (query_index != lax.broadcasted_iota(jnp.int32, cosine.shape, 1))
    weight = jnp.where(allowed, weight, 0.0)
    near = jnp.dot(weight.astype(jnp.bfloat16), unit, preferred_element_type=jnp.float32)
    return jnp.sum(weight, axis=1, keepdims=True), near


def first_kernel(core_ref, query_ref, key_ref, mass_ref, near_ref, temp_ref):
    slots, width = near_ref.shape
    temp = lane_to_row(key_ref[:, width:])
    temp_ref[...] = jnp.broadcast_to(temp, temp_ref.shape)
    mass, near = weigh(query_ref, key_ref[:, :width], temp, core_ref[0] * slots)
    mass_ref[...] = jnp.broadcast_to(mass, mass_ref.shape)
    near_ref[...] = near


def last_kernel(shift, query_ref, unit_ref, temp_ref, mass_ref, near_ref, out_ref):
    slots, width = near_ref.shape
    mass, near = weigh(query_ref, unit_ref[...], temp_ref[:1], None)
    mass = mass + mass_ref[:, :1]
    near = near + near_ref[...]
    neigh = NEIGH_SCALE * math.sqrt(width) * near / (1.0 + mass)
    mass = jnp.broadcast_to(mass, (slots, EXT))
    moved = 2 * shift
    for source, target, count in ((0, moved, slots - moved), (slots - moved, 0, moved)):
        out_ref[target : target + count, :width] = neigh[source : source + count].astype(jnp.bfloat16)
        out_ref[target : target + count, width:] = mass[source : source + count].astype(jnp.bfloat16)


def unpack_kernel(pick_ref, back_ref, neigh_ref, mass_ref):
    width = neigh_ref.shape[1]
    rows = jnp.dot(pick_ref[...], back_ref[...], preferred_element_type=jnp.float32)
    rows = rows.astype(jnp.bfloat16)
    neigh_ref[...] = rows[:, :width]
    mass_ref[...] = lane_to_row(rows[:, width:]).astype(jnp.bfloat16)


def call(kernel, outs, flops, *args, spaces=None):
    shapes = [jax.ShapeDtypeStruct(shape, dtype) for shape, dtype in outs]
    spaces = spaces or [pltpu.VMEM] * len(args)
    moved = sum(a.size * a.dtype.itemsize for a in args)
    moved += sum(math.prod(s.shape) * s.dtype.itemsize for s in shapes)
    return pl.pallas_call(
        kernel,
        out_shape=shapes,
        in_specs=[pl.BlockSpec(memory_space=space) for space in spaces],
        out_specs=[pl.BlockSpec(memory_space=pltpu.VMEM)] * len(shapes),
        compiler_params=pltpu.CompilerParams(vmem_limit_bytes=32 * 2**20),
        cost_estimate=pl.CostEstimate(flops=flops, bytes_accessed=moved, transcendentals=0),
    )(*args)


def exchange(slots, groups):
    count, wide = slots.shape
    return lax.all_to_all(
        slots.reshape(count // 2, 2, wide),
        AXES,
        split_axis=0,
        concat_axis=0,
        axis_index_groups=groups,
        tiled=True,
    )


def both_cores(rows):
    return lax.all_gather(rows, "core", axis=0, tiled=True)


def shards(layout, embeddings, inv_temp, cluster):
    rows, width = embeddings.shape
    slots = 2 * layout.count
    wide = width + EXT
    bf16, f32 = jnp.bfloat16, jnp.float32

    same, before = call(order_kernel, [((rows, rows), f32)] * 2, 8 * rows * rows * rows * rows)
    send, pick = call(
        functools.partial(pack_kernel, layout.shift),
        [((slots, wide), bf16), ((rows, slots), bf16)],
        2 * slots * rows * width,
        embeddings,
        inv_temp.reshape(1, rows),
        cluster.reshape(1, rows),
        same,
        before,
    )
    mine = exchange(send, layout.out)
    query = lax.optimization_barrier(mine.reshape(slots, wide))
    far = lax.ppermute(query[:, :width], "x", layout.pairs)
    keys = both_cores(query)
    core = lax.axis_index("core").astype(jnp.int32).reshape(1)
    work = 8 * slots * slots * width
    mass, near, temps = call(
        first_kernel,
        [((slots, EXT), f32), ((slots, width), f32), ((8, 2 * slots), f32)],
        work,
        core,
        query,
        keys,
        spaces=[pltpu.SMEM, pltpu.VMEM, pltpu.VMEM],
    )
    far_temps = lax.ppermute(temps, "x", layout.pairs)
    far_keys = both_cores(far)
    (result,) = call(
        functools.partial(last_kernel, layout.shift),
        [((slots, wide), bf16)],
        work,
        query,
        far_keys,
        far_temps,
        mass,
        near,
    )

    back = exchange(result, layout.back).reshape(slots, wide)
    neigh, dup = call(
        unpack_kernel,
        [((rows, width), bf16), ((1, rows), bf16)],
        2 * slots * rows * wide,
        pick,
        back,
    )
    return neigh, dup.reshape(rows)


def solution(mesh):
    layout = Layout(*mesh.devices.shape)
    split = Mesh(mesh.devices.reshape(layout.shape), AXES)
    return jax.shard_map(
        functools.partial(shards, layout),
        mesh=split,
        in_specs=(P(AXES, None), P(AXES), P(AXES, None)),
        out_specs=(P(AXES, None), P(AXES)),
        check_vma=False,
    )
```

```python
import functools
import math

import jax
import jax.numpy as jnp
import numpy as np
from jax import lax
from jax.experimental import pallas as pl
from jax.experimental.pallas import tpu as pltpu
from jax.sharding import Mesh
from jax.sharding import PartitionSpec as P

NEIGH_SCALE = 8.0
EXT = 128
NT = (((1,), (1,)), ((), ()))

AXES = ("z", "y", "core", "x")


class Layout:
    def __init__(self, dp, grp):
        side = math.isqrt(dp // 2)
        ids = np.arange(dp * grp).reshape(side, side, 2, grp)
        half = [[0, 3], [1, 2]]
        mid = side // 2
        steps = sorted(range(side), key=lambda step: (min(step, side - step), step))
        order = [
            ((a + b + mid) % side, (a + mid) % side, h) for b in steps for a in steps for h in (1, 0)
        ]
        first_out = order.index((side - 1, mid + 1, 1))
        first_back = order.index((mid, mid + 1, 1))
        self.count = len(order)
        self.shift = (first_out - first_back) % self.count

        def groups(start):
            return [
                [int(ids[z, y, core, half[h][s]]) for z, y, h in order[start:] + order[:start]]
                for core in range(2)
                for s in range(2)
            ]

        self.out = groups(first_out)
        self.back = groups(first_back)
        self.pairs = [(x, grp - 1 - x) for x in range(grp)]
        self.shape = ids.shape


def lane_to_row(ext):
    first = (lax.broadcasted_iota(jnp.int32, (16, EXT), 1) == 0).astype(jnp.bfloat16)
    return lax.dot_general(first, ext, NT, preferred_element_type=jnp.float32)[:1]


def order_kernel(same_ref, before_ref):
    row = lax.broadcasted_iota(jnp.int32, same_ref.shape, 0)
    col = lax.broadcasted_iota(jnp.int32, same_ref.shape, 1)
    same_ref[...] = jnp.where(row == col, 1.0, 0.0)
    before_ref[...] = jnp.where(row < col, 1.0, 0.0)


def pack_kernel(
    shift, emb_ref, temp_ref, cluster_ref, same_ref, before_ref, send_ref, pick_ref
):
    rows, width = emb_ref.shape
    slots = send_ref.shape[0]

    cluster_row = cluster_ref[...].astype(jnp.float32)
    before = before_ref[...]
    after = 1.0 - before - same_ref[...]
    cluster_col = jnp.sum(same_ref[...] * cluster_row, axis=1, keepdims=True)
    alike = cluster_row == cluster_col
    rank_row = jnp.sum(jnp.where(alike, before, 0.0), axis=0, keepdims=True)
    rank_col = jnp.sum(jnp.where(alike, after, 0.0), axis=1, keepdims=True)
    slot_row = (2.0 * cluster_row + rank_row).astype(jnp.int32)
    slot_col = (2.0 * cluster_col + rank_col).astype(jnp.int32) + 2 * shift
    slot_col = jnp.where(slot_col >= slots, slot_col - slots, slot_col)
    pick = lax.broadcasted_iota(jnp.int32, (rows, slots), 1) == slot_col
    pick_ref[...] = jnp.where(pick, 1.0, 0.0).astype(jnp.bfloat16)

    put = lax.broadcasted_iota(jnp.int32, (slots, rows), 0) == slot_row
    temp = jnp.sum(jnp.where(put, temp_ref[...].astype(jnp.float32), 0.0), axis=1, keepdims=True)
    send_ref[:, width:] = jnp.broadcast_to(temp, (slots, EXT)).astype(jnp.bfloat16)

    values = emb_ref[...].astype(jnp.float32)
    square_mean = jnp.mean(values * values, axis=1, keepdims=True)
    unit = (values * lax.rsqrt(square_mean + 1e-06) * (1.0 / math.sqrt(width))).astype(jnp.bfloat16)
    placed = jnp.dot(
        jnp.where(put, 1.0, 0.0).astype(jnp.bfloat16), unit, preferred_element_type=jnp.float32
    )
    send_ref[:, :width] = placed.astype(jnp.bfloat16)


def weigh(query_ref, unit, key_temp, own_start):
    width = unit.shape[1]
    cosine = lax.dot_general(
        query_ref[:, :width], unit, NT, preferred_element_type=jnp.float32
    )
    query_temp = query_ref[:, width : width + 1].astype(jnp.float32)
    weight = jnp.exp((cosine - 1.0) * ((query_temp + key_temp) * 0.5))
    allowed = key_temp > 0.0
    if own_start is not None:
        query_index = lax.broadcasted_iota(jnp.int32, cosine.shape, 0) + own_start
        allowed = allowed & (query_index != lax.broadcasted_iota(jnp.int32, cosine.shape, 1))
    weight = jnp.where(allowed, weight, 0.0)
    near = jnp.dot(weight.astype(jnp.bfloat16), unit, preferred_element_type=jnp.float32)
    return jnp.sum(weight, axis=1, keepdims=True), near


def first_kernel(core_ref, query_ref, key_ref, mass_ref, near_ref, temp_ref):
    slots, width = near_ref.shape
    temp = lane_to_row(key_ref[:, width:])
    temp_ref[...] = jnp.broadcast_to(temp, temp_ref.shape)
    mass, near = weigh(query_ref, key_ref[:, :width], temp, core_ref[0] * slots)
    mass_ref[...] = jnp.broadcast_to(mass, mass_ref.shape)
    near_ref[...] = near


def last_kernel(shift, query_ref, unit_ref, temp_ref, mass_ref, near_ref, out_ref):
    slots, width = near_ref.shape
    mass, near = weigh(query_ref, unit_ref[...], temp_ref[:1], None)
    mass = mass + mass_ref[:, :1]
    near = near + near_ref[...]
    neigh = NEIGH_SCALE * math.sqrt(width) * near / (1.0 + mass)
    mass = jnp.broadcast_to(mass, (slots, EXT))
    moved = 2 * shift
    for source, target, count in ((0, moved, slots - moved), (slots - moved, 0, moved)):
        out_ref[target : target + count, :width] = neigh[source : source + count].astype(jnp.bfloat16)
        out_ref[target : target + count, width:] = mass[source : source + count].astype(jnp.bfloat16)


def unpack_kernel(pick_ref, back_ref, neigh_ref, mass_ref):
    width = neigh_ref.shape[1]
    rows = jnp.dot(pick_ref[...], back_ref[...], preferred_element_type=jnp.float32)
    rows = rows.astype(jnp.bfloat16)
    neigh_ref[...] = rows[:, :width]
    mass_ref[...] = lane_to_row(rows[:, width:]).astype(jnp.bfloat16)


def call(kernel, outs, flops, *args, spaces=None):
    shapes = [jax.ShapeDtypeStruct(shape, dtype) for shape, dtype in outs]
    spaces = spaces or [pltpu.VMEM] * len(args)
    moved = sum(a.size * a.dtype.itemsize for a in args)
    moved += sum(math.prod(s.shape) * s.dtype.itemsize for s in shapes)
    return pl.pallas_call(
        kernel,
        out_shape=shapes,
        in_specs=[pl.BlockSpec(memory_space=space) for space in spaces],
        out_specs=[pl.BlockSpec(memory_space=pltpu.VMEM)] * len(shapes),
        compiler_params=pltpu.CompilerParams(vmem_limit_bytes=32 * 2**20),
        cost_estimate=pl.CostEstimate(flops=flops, bytes_accessed=moved, transcendentals=0),
    )(*args)


def exchange(slots, groups):
    count, wide = slots.shape
    return lax.all_to_all(
        slots.reshape(count // 2, 2, wide),
        AXES,
        split_axis=0,
        concat_axis=0,
        axis_index_groups=groups,
        tiled=True,
    )


def both_cores(rows):
    return lax.all_gather(rows, "core", axis=0, tiled=True)


def shards(layout, embeddings, inv_temp, cluster):
    rows, width = embeddings.shape
    slots = 2 * layout.count
    wide = width + EXT
    bf16, f32 = jnp.bfloat16, jnp.float32

    same, before = call(order_kernel, [((rows, rows), f32)] * 2, 8 * rows * rows * rows * rows)
    send, pick = call(
        functools.partial(pack_kernel, layout.shift),
        [((slots, wide), bf16), ((rows, slots), bf16)],
        2 * slots * rows * width,
        embeddings,
        inv_temp.reshape(1, rows),
        cluster.reshape(1, rows),
        same,
        before,
    )
    mine = exchange(send, layout.out)
    query = lax.optimization_barrier(mine.reshape(slots, wide))
    far = lax.ppermute(query[:, :width], "x", layout.pairs)
    keys = both_cores(query)
    core = lax.axis_index("core").astype(jnp.int32).reshape(1)
    work = 8 * slots * slots * width
    mass, near, temps = call(
        first_kernel,
        [((slots, EXT), f32), ((slots, width), f32), ((8, 2 * slots), f32)],
        work,
        core,
        query,
        keys,
        spaces=[pltpu.SMEM, pltpu.VMEM, pltpu.VMEM],
    )
    far_temps = lax.ppermute(temps, "x", layout.pairs)
    far_keys = both_cores(far)
    (result,) = call(
        functools.partial(last_kernel, layout.shift),
        [((slots, wide), bf16)],
        work,
        query,
        far_keys,
        far_temps,
        mass,
        near,
    )

    back = exchange(result, layout.back).reshape(slots, wide)
    neigh, dup = call(
        unpack_kernel,
        [((rows, width), bf16), ((1, rows), bf16)],
        2 * slots * rows * wide,
        pick,
        back,
    )
    return neigh, dup.reshape(rows)


def solution(mesh):
    layout = Layout(*mesh.devices.shape)
    split = Mesh(mesh.devices.reshape(layout.shape), AXES)
    return jax.shard_map(
        functools.partial(shards, layout),
        mesh=split,
        in_specs=(P(AXES, None), P(AXES), P(AXES, None)),
        out_specs=(P(AXES, None), P(AXES)),
        check_vma=False,
    )
```

```python
import functools
import math

import jax
import jax.numpy as jnp
import numpy as np
from jax import lax
from jax.experimental import pallas as pl
from jax.experimental.pallas import tpu as pltpu
from jax.sharding import Mesh
from jax.sharding import PartitionSpec as P

NEIGH_SCALE = 8.0
EXT = 128
NT = (((1,), (1,)), ((), ()))

AXES = ("z", "y", "core", "x")


class Layout:
    def __init__(self, dp, grp):
        side = math.isqrt(dp // 2)
        ids = np.arange(dp * grp).reshape(side, side, 2, grp)
        half = [[0, 3], [1, 2]]
        mid = side // 2
        steps = sorted(range(side), key=lambda step: (min(step, side - step), step))
        order = [
            ((a + b + mid) % side, (a + mid) % side, h) for h in range(2) for b in steps for a in steps
        ]
        first_out = order.index((side - 1, mid + 1, 0))
        first_back = order.index((mid, mid + 1, 0))
        self.count = len(order)
        self.shift = (first_out - first_back) % self.count

        def groups(start):
            return [
                [int(ids[z, y, core, half[h][s]]) for z, y, h in order[start:] + order[:start]]
                for core in range(2)
                for s in range(2)
            ]

        self.out = groups(first_out)
        self.back = groups(first_back)
        self.pairs = [(x, grp - 1 - x) for x in range(grp)]
        self.shape = ids.shape


def lane_to_row(ext):
    first = (lax.broadcasted_iota(jnp.int32, (16, EXT), 1) == 0).astype(jnp.bfloat16)
    return lax.dot_general(first, ext, NT, preferred_element_type=jnp.float32)[:1]


def order_kernel(same_ref, before_ref):
    row = lax.broadcasted_iota(jnp.int32, same_ref.shape, 0)
    col = lax.broadcasted_iota(jnp.int32, same_ref.shape, 1)
    same_ref[...] = jnp.where(row == col, 1.0, 0.0)
    before_ref[...] = jnp.where(row < col, 1.0, 0.0)


def pack_kernel(
    shift, emb_ref, temp_ref, cluster_ref, same_ref, before_ref, send_ref, pick_ref
):
    rows, width = emb_ref.shape
    slots = pick_ref.shape[1]

    cluster_row = cluster_ref[...].astype(jnp.float32)
    before = before_ref[...]
    after = 1.0 - before - same_ref[...]
    cluster_col = jnp.sum(same_ref[...] * cluster_row, axis=1, keepdims=True)
    alike = cluster_row == cluster_col
    rank_row = jnp.sum(jnp.where(alike, before, 0.0), axis=0, keepdims=True)
    rank_col = jnp.sum(jnp.where(alike, after, 0.0), axis=1, keepdims=True)
    slot_row = (2.0 * cluster_row + rank_row).astype(jnp.int32)
    slot_col = (2.0 * cluster_col + rank_col).astype(jnp.int32) + 2 * shift
    slot_col = jnp.where(slot_col >= slots, slot_col - slots, slot_col)
    pick = lax.broadcasted_iota(jnp.int32, (rows, slots), 1) == slot_col
    pick_ref[...] = jnp.where(pick, 1.0, 0.0).astype(jnp.bfloat16)

    put = lax.broadcasted_iota(jnp.int32, (slots, rows), 0) == slot_row
    temp = jnp.sum(jnp.where(put, temp_ref[...].astype(jnp.float32), 0.0), axis=1, keepdims=True)
    temp = jnp.broadcast_to(temp, (slots, EXT)).astype(jnp.bfloat16)
    send_ref[:, :, width:] = temp.reshape(slots // 2, 2, EXT)

    values = emb_ref[...].astype(jnp.float32)
    square_mean = jnp.mean(values * values, axis=1, keepdims=True)
    unit = (values * lax.rsqrt(square_mean + 1e-06) * (1.0 / math.sqrt(width))).astype(jnp.bfloat16)
    placed = jnp.dot(
        jnp.where(put, 1.0, 0.0).astype(jnp.bfloat16), unit, preferred_element_type=jnp.float32
    )
    send_ref[:, :, :width] = placed.astype(jnp.bfloat16).reshape(slots // 2, 2, width)


def weigh(query_ref, unit, key_temp, own_start):
    width = unit.shape[1]
    cosine = lax.dot_general(
        query_ref[:, :width], unit, NT, preferred_element_type=jnp.float32
    )
    query_temp = query_ref[:, width : width + 1].astype(jnp.float32)
    weight = jnp.exp((cosine - 1.0) * ((query_temp + key_temp) * 0.5))
    allowed = key_temp > 0.0
    if own_start is not None:
        query_index = lax.broadcasted_iota(jnp.int32, cosine.shape, 0) + own_start
        allowed = allowed & (query_index != lax.broadcasted_iota(jnp.int32, cosine.shape, 1))
    weight = jnp.where(allowed, weight, 0.0)
    near = jnp.dot(weight.astype(jnp.bfloat16), unit, preferred_element_type=jnp.float32)
    return jnp.sum(weight, axis=1, keepdims=True), near


def first_kernel(core_ref, query_ref, key_ref, mass_ref, near_ref, temp_ref):
    slots, width = near_ref.shape
    temp = lane_to_row(key_ref[:, width:])
    temp_ref[...] = jnp.broadcast_to(temp, temp_ref.shape)
    mass, near = weigh(query_ref, key_ref[:, :width], temp, core_ref[0] * slots)
    mass_ref[...] = jnp.broadcast_to(mass, mass_ref.shape)
    near_ref[...] = near


def last_kernel(shift, query_ref, unit_ref, temp_ref, mass_ref, near_ref, out_ref):
    slots, width = near_ref.shape
    mass, near = weigh(query_ref, unit_ref[...], temp_ref[:1], None)
    mass = mass + mass_ref[:, :1]
    near = near + near_ref[...]
    neigh = NEIGH_SCALE * math.sqrt(width) * near / (1.0 + mass)
    mass = jnp.broadcast_to(mass, (slots, EXT))
    moved = 2 * shift
    for source, target, count in ((0, moved, slots - moved), (slots - moved, 0, moved)):
        pairs = pl.ds(target // 2, count // 2)
        for values, columns in ((neigh, slice(0, width)), (mass, slice(width, width + EXT))):
            part = values[source : source + count].astype(jnp.bfloat16)
            out_ref[pairs, :, columns] = part.reshape(count // 2, 2, part.shape[1])


def unpack_kernel(pick_ref, back_ref, neigh_ref, mass_ref):
    width = neigh_ref.shape[1]
    back = back_ref[...].reshape(pick_ref.shape[1], back_ref.shape[2])
    rows = jnp.dot(pick_ref[...], back, preferred_element_type=jnp.float32)
    rows = rows.astype(jnp.bfloat16)
    neigh_ref[...] = rows[:, :width]
    mass_ref[...] = lane_to_row(rows[:, width:]).astype(jnp.bfloat16)


def call(kernel, outs, flops, *args, spaces=None):
    shapes = [jax.ShapeDtypeStruct(shape, dtype) for shape, dtype in outs]
    spaces = spaces or [pltpu.VMEM] * len(args)
    moved = sum(a.size * a.dtype.itemsize for a in args)
    moved += sum(math.prod(s.shape) * s.dtype.itemsize for s in shapes)
    return pl.pallas_call(
        kernel,
        out_shape=shapes,
        in_specs=[pl.BlockSpec(memory_space=space) for space in spaces],
        out_specs=[pl.BlockSpec(memory_space=pltpu.VMEM)] * len(shapes),
        compiler_params=pltpu.CompilerParams(vmem_limit_bytes=32 * 2**20),
        cost_estimate=pl.CostEstimate(flops=flops, bytes_accessed=moved, transcendentals=0),
    )(*args)


def exchange(pairs, groups):
    return lax.all_to_all(
        pairs, AXES, split_axis=0, concat_axis=0, axis_index_groups=groups, tiled=True
    )


def both_cores(rows):
    return lax.all_gather(rows, "core", axis=0, tiled=True)


def shards(layout, embeddings, inv_temp, cluster):
    rows, width = embeddings.shape
    slots = 2 * layout.count
    wide = width + EXT
    bf16, f32 = jnp.bfloat16, jnp.float32

    same, before = call(order_kernel, [((rows, rows), f32)] * 2, 8 * rows * rows * rows * rows)
    send, pick = call(
        functools.partial(pack_kernel, layout.shift),
        [((slots // 2, 2, wide), bf16), ((rows, slots), bf16)],
        2 * slots * rows * width,
        embeddings,
        inv_temp.reshape(1, rows),
        cluster.reshape(1, rows),
        same,
        before,
    )
    mine = exchange(send, layout.out)
    query = lax.optimization_barrier(mine.reshape(slots, wide))
    far = lax.ppermute(query[:, :width], "x", layout.pairs)
    keys = both_cores(query)
    core = lax.axis_index("core").astype(jnp.int32).reshape(1)
    work = 8 * slots * slots * width
    mass, near, temps = call(
        first_kernel,
        [((slots, EXT), f32), ((slots, width), f32), ((8, 2 * slots), f32)],
        work,
        core,
        query,
        keys,
        spaces=[pltpu.SMEM, pltpu.VMEM, pltpu.VMEM],
    )
    far_temps = lax.ppermute(temps, "x", layout.pairs)
    far_keys = both_cores(far)
    (result,) = call(
        functools.partial(last_kernel, layout.shift),
        [((slots // 2, 2, wide), bf16)],
        work,
        query,
        far_keys,
        far_temps,
        mass,
        near,
    )

    back = exchange(result, layout.back)
    neigh, dup = call(
        unpack_kernel,
        [((rows, width), bf16), ((1, rows), bf16)],
        2 * slots * rows * wide,
        pick,
        back,
    )
    return neigh, dup.reshape(rows)


def solution(mesh):
    layout = Layout(*mesh.devices.shape)
    split = Mesh(mesh.devices.reshape(layout.shape), AXES)
    return jax.shard_map(
        functools.partial(shards, layout),
        mesh=split,
        in_specs=(P(AXES, None), P(AXES), P(AXES, None)),
        out_specs=(P(AXES, None), P(AXES)),
        check_vma=False,
    )
```

```python
import functools
import math

import jax
import jax.numpy as jnp
import numpy as np
from jax import lax
from jax.experimental import pallas as pl
from jax.experimental.pallas import tpu as pltpu
from jax.sharding import Mesh
from jax.sharding import PartitionSpec as P

NEIGH_SCALE = 8.0
EXT = 128
NT = (((1,), (1,)), ((), ()))

AXES = ("z", "y", "core", "x")


class Layout:
    def __init__(self, dp, grp):
        side = math.isqrt(dp // 2)
        ids = np.arange(dp * grp).reshape(side, side, 2, grp)
        half = [[0, 3], [1, 2]]
        mid = side // 2
        steps = sorted(range(side), key=lambda step: (min(step, side - step), step))
        order = [
            ((a + b + mid) % side, (a + mid) % side, h) for h in range(2) for b in steps for a in steps
        ]
        first_out = order.index((side - 1, mid, 0))
        first_back = order.index((mid, mid + 1, 0))
        apart = (first_back - first_out) % 8
        order[first_out], order[first_out + apart] = order[first_out + apart], order[first_out]
        first_out += apart
        self.count = len(order)
        self.shift = (first_out - first_back) % self.count

        def groups(start):
            return [
                [int(ids[z, y, core, half[h][s]]) for z, y, h in order[start:] + order[:start]]
                for core in range(2)
                for s in range(2)
            ]

        self.out = groups(first_out)
        self.back = groups(first_back)
        self.pairs = [(x, grp - 1 - x) for x in range(grp)]
        self.shape = ids.shape


def lane_to_row(ext):
    first = (lax.broadcasted_iota(jnp.int32, (16, EXT), 1) == 0).astype(jnp.bfloat16)
    return lax.dot_general(first, ext, NT, preferred_element_type=jnp.float32)[:1]


def order_kernel(same_ref, before_ref):
    row = lax.broadcasted_iota(jnp.int32, same_ref.shape, 0)
    col = lax.broadcasted_iota(jnp.int32, same_ref.shape, 1)
    same_ref[...] = jnp.where(row == col, 1.0, 0.0)
    before_ref[...] = jnp.where(row < col, 1.0, 0.0)


def pack_kernel(
    shift, emb_ref, temp_ref, cluster_ref, same_ref, before_ref, send_ref, pick_ref
):
    rows, width = emb_ref.shape
    slots = pick_ref.shape[1]

    cluster_row = cluster_ref[...].astype(jnp.float32)
    before = before_ref[...]
    after = 1.0 - before - same_ref[...]
    cluster_col = jnp.sum(same_ref[...] * cluster_row, axis=1, keepdims=True)
    alike = cluster_row == cluster_col
    rank_row = jnp.sum(jnp.where(alike, before, 0.0), axis=0, keepdims=True)
    rank_col = jnp.sum(jnp.where(alike, after, 0.0), axis=1, keepdims=True)
    slot_row = (2.0 * cluster_row + rank_row).astype(jnp.int32)
    slot_col = (2.0 * cluster_col + rank_col).astype(jnp.int32) + 2 * shift
    slot_col = jnp.where(slot_col >= slots, slot_col - slots, slot_col)
    pick = lax.broadcasted_iota(jnp.int32, (rows, slots), 1) == slot_col
    pick_ref[...] = jnp.where(pick, 1.0, 0.0).astype(jnp.bfloat16)

    put = lax.broadcasted_iota(jnp.int32, (slots, rows), 0) == slot_row
    temp = jnp.sum(jnp.where(put, temp_ref[...].astype(jnp.float32), 0.0), axis=1, keepdims=True)
    temp = jnp.broadcast_to(temp, (slots, EXT)).astype(jnp.bfloat16)
    send_ref[:, :, width:] = temp.reshape(slots // 2, 2, EXT)

    values = emb_ref[...].astype(jnp.float32)
    square_mean = jnp.mean(values * values, axis=1, keepdims=True)
    unit = (values * lax.rsqrt(square_mean + 1e-06) * (1.0 / math.sqrt(width))).astype(jnp.bfloat16)
    placed = jnp.dot(
        jnp.where(put, 1.0, 0.0).astype(jnp.bfloat16), unit, preferred_element_type=jnp.float32
    )
    send_ref[:, :, :width] = placed.astype(jnp.bfloat16).reshape(slots // 2, 2, width)


def weigh(query_ref, unit, key_temp, own_start):
    width = unit.shape[1]
    cosine = lax.dot_general(
        query_ref[:, :width], unit, NT, preferred_element_type=jnp.float32
    )
    query_temp = query_ref[:, width : width + 1].astype(jnp.float32)
    weight = jnp.exp((cosine - 1.0) * ((query_temp + key_temp) * 0.5))
    allowed = key_temp > 0.0
    if own_start is not None:
        query_index = lax.broadcasted_iota(jnp.int32, cosine.shape, 0) + own_start
        allowed = allowed & (query_index != lax.broadcasted_iota(jnp.int32, cosine.shape, 1))
    weight = jnp.where(allowed, weight, 0.0)
    near = jnp.dot(weight.astype(jnp.bfloat16), unit, preferred_element_type=jnp.float32)
    return jnp.sum(weight, axis=1, keepdims=True), near


def first_kernel(core_ref, query_ref, key_ref, mass_ref, near_ref, temp_ref):
    slots, width = near_ref.shape
    temp = lane_to_row(key_ref[:, width:])
    temp_ref[...] = jnp.broadcast_to(temp, temp_ref.shape)
    mass, near = weigh(query_ref, key_ref[:, :width], temp, core_ref[0] * slots)
    mass_ref[...] = jnp.broadcast_to(mass, mass_ref.shape)
    near_ref[...] = near


def last_kernel(shift, query_ref, unit_ref, temp_ref, mass_ref, near_ref, out_ref):
    slots, width = near_ref.shape
    mass, near = weigh(query_ref, unit_ref[...], temp_ref[:1], None)
    mass = mass + mass_ref[:, :1]
    near = near + near_ref[...]
    neigh = NEIGH_SCALE * math.sqrt(width) * near / (1.0 + mass)
    mass = jnp.broadcast_to(mass, (slots, EXT))
    moved = 2 * shift
    for source, target, count in ((0, moved, slots - moved), (slots - moved, 0, moved)):
        pairs = pl.ds(target // 2, count // 2)
        for values, columns in ((neigh, slice(0, width)), (mass, slice(width, width + EXT))):
            part = values[source : source + count].astype(jnp.bfloat16)
            out_ref[pairs, :, columns] = part.reshape(count // 2, 2, part.shape[1])


def unpack_kernel(pick_ref, back_ref, neigh_ref, mass_ref):
    width = neigh_ref.shape[1]
    back = back_ref[...].reshape(pick_ref.shape[1], back_ref.shape[2])
    rows = jnp.dot(pick_ref[...], back, preferred_element_type=jnp.float32)
    rows = rows.astype(jnp.bfloat16)
    neigh_ref[...] = rows[:, :width]
    mass_ref[...] = lane_to_row(rows[:, width:]).astype(jnp.bfloat16)


def call(kernel, outs, flops, *args, spaces=None):
    shapes = [jax.ShapeDtypeStruct(shape, dtype) for shape, dtype in outs]
    spaces = spaces or [pltpu.VMEM] * len(args)
    moved = sum(a.size * a.dtype.itemsize for a in args)
    moved += sum(math.prod(s.shape) * s.dtype.itemsize for s in shapes)
    return pl.pallas_call(
        kernel,
        out_shape=shapes,
        in_specs=[pl.BlockSpec(memory_space=space) for space in spaces],
        out_specs=[pl.BlockSpec(memory_space=pltpu.VMEM)] * len(shapes),
        compiler_params=pltpu.CompilerParams(vmem_limit_bytes=32 * 2**20),
        cost_estimate=pl.CostEstimate(flops=flops, bytes_accessed=moved, transcendentals=0),
    )(*args)


def exchange(pairs, groups):
    return lax.all_to_all(
        pairs, AXES, split_axis=0, concat_axis=0, axis_index_groups=groups, tiled=True
    )


def both_cores(rows):
    return lax.all_gather(rows, "core", axis=0, tiled=True)


def shards(layout, embeddings, inv_temp, cluster):
    rows, width = embeddings.shape
    slots = 2 * layout.count
    wide = width + EXT
    bf16, f32 = jnp.bfloat16, jnp.float32

    same, before = call(order_kernel, [((rows, rows), f32)] * 2, 8 * rows * rows * rows * rows)
    send, pick = call(
        functools.partial(pack_kernel, layout.shift),
        [((slots // 2, 2, wide), bf16), ((rows, slots), bf16)],
        2 * slots * rows * width,
        embeddings,
        inv_temp.reshape(1, rows),
        cluster.reshape(1, rows),
        same,
        before,
    )
    mine = exchange(send, layout.out)
    query = lax.optimization_barrier(mine.reshape(slots, wide))
    far = lax.ppermute(query[:, :width], "x", layout.pairs)
    keys = both_cores(query)
    core = lax.axis_index("core").astype(jnp.int32).reshape(1)
    work = 8 * slots * slots * width
    mass, near, temps = call(
        first_kernel,
        [((slots, EXT), f32), ((slots, width), f32), ((8, 2 * slots), f32)],
        work,
        core,
        query,
        keys,
        spaces=[pltpu.SMEM, pltpu.VMEM, pltpu.VMEM],
    )
    far_temps = lax.ppermute(temps, "x", layout.pairs)
    far_keys = both_cores(far)
    (result,) = call(
        functools.partial(last_kernel, layout.shift),
        [((slots // 2, 2, wide), bf16)],
        work,
        query,
        far_keys,
        far_temps,
        mass,
        near,
    )

    back = exchange(result, layout.back)
    neigh, dup = call(
        unpack_kernel,
        [((rows, width), bf16), ((1, rows), bf16)],
        2 * slots * rows * wide,
        pick,
        back,
    )
    return neigh, dup.reshape(rows)


def solution(mesh):
    layout = Layout(*mesh.devices.shape)
    split = Mesh(mesh.devices.reshape(layout.shape), AXES)
    return jax.shard_map(
        functools.partial(shards, layout),
        mesh=split,
        in_specs=(P(AXES, None), P(AXES), P(AXES, None)),
        out_specs=(P(AXES, None), P(AXES)),
        check_vma=False,
    )
```

```python
import functools
import math

import jax
import jax.numpy as jnp
import numpy as np
from jax import lax
from jax.experimental import pallas as pl
from jax.experimental.pallas import tpu as pltpu
from jax.sharding import Mesh
from jax.sharding import PartitionSpec as P

NEIGH_SCALE = 8.0
EXT = 128
NT = (((1,), (1,)), ((), ()))

AXES = ("z", "y", "core", "x")


class Layout:
    def __init__(self, dp, grp):
        side = math.isqrt(dp // 2)
        ids = np.arange(dp * grp).reshape(side, side, 2, grp)
        half = [[0, 3], [1, 2]]
        mid = side // 2
        steps = sorted(range(side), key=lambda step: (min(step, side - step), step))
        order = [
            ((a + b + mid) % side, (a + mid) % side, h) for h in range(2) for b in steps for a in steps
        ]
        first_out = order.index((side - 1, mid + 2, 0))
        first_back = order.index((mid, mid + 2, 0))
        self.count = len(order)
        self.shift = (first_out - first_back) % self.count

        def groups(start):
            return [
                [int(ids[z, y, core, half[h][s]]) for z, y, h in order[start:] + order[:start]]
                for core in range(2)
                for s in range(2)
            ]

        self.out = groups(first_out)
        self.back = groups(first_back)
        self.pairs = [(x, grp - 1 - x) for x in range(grp)]
        self.shape = ids.shape


def lane_to_row(ext):
    first = (lax.broadcasted_iota(jnp.int32, (16, EXT), 1) == 0).astype(jnp.bfloat16)
    return lax.dot_general(first, ext, NT, preferred_element_type=jnp.float32)[:1]


def order_kernel(same_ref, before_ref):
    row = lax.broadcasted_iota(jnp.int32, same_ref.shape, 0)
    col = lax.broadcasted_iota(jnp.int32, same_ref.shape, 1)
    same_ref[...] = jnp.where(row == col, 1.0, 0.0)
    before_ref[...] = jnp.where(row < col, 1.0, 0.0)


def pack_kernel(
    shift, emb_ref, temp_ref, cluster_ref, same_ref, before_ref, send_ref, pick_ref
):
    rows, width = emb_ref.shape
    slots = pick_ref.shape[1]

    cluster_row = cluster_ref[...].astype(jnp.float32)
    before = before_ref[...]
    after = 1.0 - before - same_ref[...]
    cluster_col = jnp.sum(same_ref[...] * cluster_row, axis=1, keepdims=True)
    alike = cluster_row == cluster_col
    rank_row = jnp.sum(jnp.where(alike, before, 0.0), axis=0, keepdims=True)
    rank_col = jnp.sum(jnp.where(alike, after, 0.0), axis=1, keepdims=True)
    slot_row = (2.0 * cluster_row + rank_row).astype(jnp.int32)
    slot_col = (2.0 * cluster_col + rank_col).astype(jnp.int32) + 2 * shift
    slot_col = jnp.where(slot_col >= slots, slot_col - slots, slot_col)
    pick = lax.broadcasted_iota(jnp.int32, (rows, slots), 1) == slot_col
    pick_ref[...] = jnp.where(pick, 1.0, 0.0).astype(jnp.bfloat16)

    put = lax.broadcasted_iota(jnp.int32, (slots, rows), 0) == slot_row
    temp = jnp.sum(jnp.where(put, temp_ref[...].astype(jnp.float32), 0.0), axis=1, keepdims=True)
    temp = jnp.broadcast_to(temp, (slots, EXT)).astype(jnp.bfloat16)
    send_ref[:, :, width:] = temp.reshape(slots // 2, 2, EXT)

    values = emb_ref[...].astype(jnp.float32)
    square_mean = jnp.mean(values * values, axis=1, keepdims=True)
    unit = (values * lax.rsqrt(square_mean + 1e-06) * (1.0 / math.sqrt(width))).astype(jnp.bfloat16)
    placed = jnp.dot(
        jnp.where(put, 1.0, 0.0).astype(jnp.bfloat16), unit, preferred_element_type=jnp.float32
    )
    send_ref[:, :, :width] = placed.astype(jnp.bfloat16).reshape(slots // 2, 2, width)


def weigh(query_ref, unit, key_temp, own_start):
    width = unit.shape[1]
    cosine = lax.dot_general(
        query_ref[:, :width], unit, NT, preferred_element_type=jnp.float32
    )
    query_temp = query_ref[:, width : width + 1].astype(jnp.float32)
    weight = jnp.exp((cosine - 1.0) * ((query_temp + key_temp) * 0.5))
    allowed = key_temp > 0.0
    if own_start is not None:
        query_index = lax.broadcasted_iota(jnp.int32, cosine.shape, 0) + own_start
        allowed = allowed & (query_index != lax.broadcasted_iota(jnp.int32, cosine.shape, 1))
    weight = jnp.where(allowed, weight, 0.0)
    near = jnp.dot(weight.astype(jnp.bfloat16), unit, preferred_element_type=jnp.float32)
    return jnp.sum(weight, axis=1, keepdims=True), near


def first_kernel(core_ref, query_ref, key_ref, mass_ref, near_ref, temp_ref):
    slots, width = near_ref.shape
    temp = lane_to_row(key_ref[:, width:])
    temp_ref[...] = jnp.broadcast_to(temp, temp_ref.shape)
    mass, near = weigh(query_ref, key_ref[:, :width], temp, core_ref[0] * slots)
    mass_ref[...] = jnp.broadcast_to(mass, mass_ref.shape)
    near_ref[...] = near


def last_kernel(shift, query_ref, unit_ref, temp_ref, mass_ref, near_ref, out_ref):
    slots, width = near_ref.shape
    mass, near = weigh(query_ref, unit_ref[...], temp_ref[:1], None)
    mass = mass + mass_ref[:, :1]
    near = near + near_ref[...]
    neigh = NEIGH_SCALE * math.sqrt(width) * near / (1.0 + mass)
    mass = jnp.broadcast_to(mass, (slots, EXT))
    moved = 2 * shift
    for source, target, count in ((0, moved, slots - moved), (slots - moved, 0, moved)):
        pairs = pl.ds(target // 2, count // 2)
        for values, columns in ((neigh, slice(0, width)), (mass, slice(width, width + EXT))):
            part = values[source : source + count].astype(jnp.bfloat16)
            out_ref[pairs, :, columns] = part.reshape(count // 2, 2, part.shape[1])


def unpack_kernel(pick_ref, back_ref, neigh_ref, mass_ref):
    width = neigh_ref.shape[1]
    back = back_ref[...].reshape(pick_ref.shape[1], back_ref.shape[2])
    rows = jnp.dot(pick_ref[...], back, preferred_element_type=jnp.float32)
    rows = rows.astype(jnp.bfloat16)
    neigh_ref[...] = rows[:, :width]
    mass_ref[...] = lane_to_row(rows[:, width:]).astype(jnp.bfloat16)


def call(kernel, outs, flops, *args, spaces=None):
    shapes = [jax.ShapeDtypeStruct(shape, dtype) for shape, dtype in outs]
    spaces = spaces or [pltpu.VMEM] * len(args)
    moved = sum(a.size * a.dtype.itemsize for a in args)
    moved += sum(math.prod(s.shape) * s.dtype.itemsize for s in shapes)
    return pl.pallas_call(
        kernel,
        out_shape=shapes,
        in_specs=[pl.BlockSpec(memory_space=space) for space in spaces],
        out_specs=[pl.BlockSpec(memory_space=pltpu.VMEM)] * len(shapes),
        compiler_params=pltpu.CompilerParams(vmem_limit_bytes=32 * 2**20),
        cost_estimate=pl.CostEstimate(flops=flops, bytes_accessed=moved, transcendentals=0),
    )(*args)


def exchange(pairs, groups):
    return lax.all_to_all(
        pairs, AXES, split_axis=0, concat_axis=0, axis_index_groups=groups, tiled=True
    )


def both_cores(rows):
    return lax.all_gather(rows, "core", axis=0, tiled=True)


def shards(layout, embeddings, inv_temp, cluster):
    rows, width = embeddings.shape
    slots = 2 * layout.count
    wide = width + EXT
    bf16, f32 = jnp.bfloat16, jnp.float32

    same, before = call(order_kernel, [((rows, rows), f32)] * 2, 8 * rows * rows * rows * rows)
    send, pick = call(
        functools.partial(pack_kernel, layout.shift),
        [((slots // 2, 2, wide), bf16), ((rows, slots), bf16)],
        2 * slots * rows * width,
        embeddings,
        inv_temp.reshape(1, rows),
        cluster.reshape(1, rows),
        same,
        before,
    )
    mine = exchange(send, layout.out)
    query = lax.optimization_barrier(mine.reshape(slots, wide))
    far = lax.ppermute(query[:, :width], "x", layout.pairs)
    keys = both_cores(query)
    core = lax.axis_index("core").astype(jnp.int32).reshape(1)
    work = 8 * slots * slots * width
    mass, near, temps = call(
        first_kernel,
        [((slots, EXT), f32), ((slots, width), f32), ((8, 2 * slots), f32)],
        work,
        core,
        query,
        keys,
        spaces=[pltpu.SMEM, pltpu.VMEM, pltpu.VMEM],
    )
    far_temps = lax.ppermute(temps, "x", layout.pairs)
    far_keys = both_cores(far)
    (result,) = call(
        functools.partial(last_kernel, layout.shift),
        [((slots // 2, 2, wide), bf16)],
        work,
        query,
        far_keys,
        far_temps,
        mass,
        near,
    )

    back = exchange(result, layout.back)
    neigh, dup = call(
        unpack_kernel,
        [((rows, width), bf16), ((1, rows), bf16)],
        2 * slots * rows * wide,
        pick,
        back,
    )
    return neigh, dup.reshape(rows)


def solution(mesh):
    layout = Layout(*mesh.devices.shape)
    split = Mesh(mesh.devices.reshape(layout.shape), AXES)
    return jax.shard_map(
        functools.partial(shards, layout),
        mesh=split,
        in_specs=(P(AXES, None), P(AXES), P(AXES, None)),
        out_specs=(P(AXES, None), P(AXES)),
        check_vma=False,
    )
```
